128 devices in a mesh: geno: 16 (over y, z_lo, core), trial: 8 (over x, z_hi).
Axes of the slice: x: 4, y: 4, z: 4 (z_hi: 2, z_lo: 2; z = z_hi * 2 + z_lo), core: 2. Of those that a mesh axis runs over, the one named last changes fastest.
Arguments:
- right_side: float32 [12288, 1, 2048], P('geno', None, 'trial'), may hold values from -6 to 6
- observed: int32 [12288, 2048], P('geno', 'trial'), may hold values from 0 to 1, as said below
- row_length: int32 [2048], P('trial'), may hold values from 2 to 16
- field_coef: float32 [2048], P('trial'), may hold values from 0.5 to 4
- kernel_geno: bfloat16 [12288, 12288], P('geno'), may hold values from -1 to 3, as said below
- kernel_trial: bfloat16 [2048, 2048], P('trial'), may hold values from -1 to 3, as said below
Outputs:
- solution_field: float32 [12288, 1, 2048], P('geno', None, 'trial')
- residual: float32 [12288, 1, 2048], P('geno', None, 'trial')
The draws below stay inside these ranges and needn't reach their ends.
Inputs may be any that keep to these rules, and one draw needn't show every extreme that they name: kernel_geno is symmetric. kernel_trial is symmetric. 1 marks an observed cell, 0 a missing one.
All inputs are finite; a program needn't handle non-finite values.
Results may differ from the reference program's by a relative error of at most 0.0028.
Values may be sent and summed in bfloat16 or wider, within the bound.
No kernel may reach another device: no remote copies, remote signals or barrier semaphores. Data moves between devices by JAX's collectives and lax.ppermute only.
A program may use at most 128 MiB of HBM per device.

```python
import math
import jax
import jax.numpy as jnp

G = 12288
E = 2048
R = 1
ITERS = 2


def region_levels(key):
    key = jax.random.fold_in(key, 11)
    level = jnp.zeros((G,), jnp.int32)
    for depth, weight in ((1, 2), (2, 1), (3, 1)):
        count = 2 ** depth
        signs = jax.random.randint(jax.random.fold_in(key, depth), (count,), 0, 2) * 2 - 1
        level = level + weight * jnp.repeat(signs, G // count, total_repeat_length=G)
    return level


def symmetric_kernel(key, order, diag_vals):
    noise = jnp.clip(jax.random.normal(key, (order, order), jnp.float32), -6.0, 6.0)
    off_part = (noise + noise.T) * (0.5 / jnp.sqrt(2.0 * order))
    eye_mask = (jnp.arange(order)[:, None] == jnp.arange(order)[None, :]).astype(jnp.float32)
    kernel = off_part * (1.0 - eye_mask) + eye_mask * diag_vals[None, :]
    return kernel.astype(jnp.bfloat16)


def draw_kernel_geno(key, part):
    level = region_levels(key).astype(jnp.float32)
    key = jax.random.fold_in(key, 1)
    first, second = jax.random.split(key)
    jitter = jax.random.uniform(second, (G,), jnp.float32, -0.1, 0.1)
    diag_vals = 1.9 + 0.225 * level + jitter
    return symmetric_kernel(first, G, diag_vals)


def draw_kernel_trial(key, part):
    key = jax.random.fold_in(key, 2)
    first, second = jax.random.split(key)
    diag_vals = jax.random.uniform(second, (E,), jnp.float32, 1.5, 2.5)
    return symmetric_kernel(first, E, diag_vals)


def draw_observed(key, part):
    row_rates = 5 + region_levels(key)
    key = jax.random.fold_in(key, 3)
    first, second = jax.random.split(key)
    trial_rates = jax.random.randint(first, (E,), 1, 10)
    cells = jax.random.randint(second, (G, E), 0, 81)
    return (cells < row_rates[:, None] * trial_rates[None, :]).astype(jnp.int32)


def touch_ends(values, key, smallest, top_value):
    longest = values.shape.index(max(values.shape))
    spots = []
    for shift in (0, 1):
        where = [jax.random.randint(jax.random.fold_in(key, axis), (), 0, length) for axis, length in enumerate(values.shape)]
        where[longest] = (where[longest] + shift) % values.shape[longest]
        spots.append(tuple(where))
    return values.at[spots[0]].set(smallest).at[spots[1]].set(top_value)


def steps_of(rng, dims, pieces, least, high):
    loudness = 1.0
    for axis_at, blocks in pieces:
        steps = jax.random.uniform(jax.random.fold_in(jax.random.fold_in(rng, 6), axis_at), (blocks,), jnp.float32, least / len(pieces), high / len(pieces))
        loudness = loudness * jnp.repeat(jnp.exp(steps), dims[axis_at] // blocks).reshape((-1,) + (1,) * (len(dims) - 1 - axis_at))
    return loudness


def gaussian(rng, shape, deviation, bound, pieces=(), kind=jnp.bfloat16):
    gain = steps_of(rng, shape, pieces, -0.22, 0.18) if pieces else 1.0
    result = jax.random.normal(rng, shape, jnp.float32) * deviation * gain
    return jnp.minimum(jnp.maximum(result, -bound), bound).astype(kind)


def setup_inputs(seed: int = 0) -> dict:
    key_list = jax.random.split(jax.random.key(seed), 7)
    return {
        "right_side": gaussian(key_list[0], (G, R, E), 1.0, 6.0, ((0, 16), (2, 8)), jnp.float32),
        "observed": draw_observed(jax.random.fold_in(key_list[6], 71), 0),
        "row_length": touch_ends(jax.random.randint(key_list[2], (E,), 2, 17), jax.random.fold_in(key_list[2], 1), 2, 16).astype(jnp.int32),
        "field_coef": jnp.clip(jnp.exp(math.log(4.0) - 2.0794415 * jax.random.uniform(key_list[3], (E,), jnp.float32) ** steps_of(key_list[3], (E,), ((0, 8),), -0.2, 0.2)), 0.5, 4.0),
        "kernel_geno": draw_kernel_geno(jax.random.fold_in(key_list[6], 71), 0),
        "kernel_trial": draw_kernel_trial(jax.random.fold_in(key_list[6], 71), 0),
    }


def field_links(row_length):
    position = jnp.arange(-1, G, dtype=jnp.int32)[:, None]
    keep = (position >= 0) & (position + 1 < G) & (((position + 1) % row_length[None, :]) != 0)
    return keep.astype(jnp.float32)[:, None, :]


def operate(vector, observed_f, links, coef, kernel_geno, kernel_trial):
    masked = (observed_f * vector).astype(jnp.bfloat16)
    mixed = jnp.dot(kernel_geno, masked.reshape(G, R * E), preferred_element_type=jnp.float32)
    mixed = mixed.astype(jnp.bfloat16).reshape(G * R, E)
    crossed = jnp.dot(mixed, kernel_trial, preferred_element_type=jnp.float32).reshape(G, R, E)
    zero_row = jnp.zeros((1, R, E), jnp.float32)
    padded = jnp.concatenate([zero_row, vector, zero_row], axis=0)
    flux = links * (padded[1:] - padded[:-1])
    field = vector - coef * (flux[1:] - flux[:-1])
    return observed_f * crossed + field


def reference(right_side, observed, row_length, field_coef, kernel_geno, kernel_trial):
    observed_f = observed.astype(jnp.float32)[:, None, :]
    links = field_links(row_length)
    coef = field_coef[None, None, :]
    solution_field = jnp.zeros_like(right_side)
    residual = right_side
    direction = right_side
    norm_now = jnp.sum(residual * residual, axis=(0, 2))
    for step in range(ITERS):
        image = operate(direction, observed_f, links, coef, kernel_geno, kernel_trial)
        alpha = (norm_now / jnp.sum(direction * image, axis=(0, 2)))[None, :, None]
        solution_field = solution_field + alpha * direction
        residual = residual - alpha * image
        norm_next = jnp.sum(residual * residual, axis=(0, 2))
        direction = residual + (norm_next / norm_now)[None, :, None] * direction
        norm_now = norm_next
    return solution_field, residual
```

```python
import jax
import jax.numpy as jnp
from jax import lax
from jax.experimental import pallas as pl
from jax.experimental.pallas import tpu as pltpu
from jax.sharding import PartitionSpec as P

BOTH = ("geno", "trial")
RING, PAIR, CORES = 4, 2, 2
F32, BF16 = jnp.float32, jnp.bfloat16
SMEM = pl.BlockSpec(memory_space=pltpu.SMEM)
VMEM = pl.BlockSpec(memory_space=pltpu.VMEM)
ANY = pl.BlockSpec(memory_space=pl.ANY)
HBM = pl.BlockSpec(memory_space=pltpu.HBM)


def place(index):
    geno, trial = divmod(index, RING * PAIR)
    return (geno // 4, geno // 2 % 2, geno % 2, trial // 2, trial % 2)


def hop(cells, **by):
    step = [by.get(name, 0) for name in ("y", "z", "core", "x", "far")]
    pairs = []
    for index in range(RING * PAIR * CORES * RING * PAIR):
        y, z, core, x, far = (a + b for a, b in zip(place(index), step))
        geno = ((y % RING) * PAIR + z % PAIR) * CORES + core % CORES
        pairs.append((index, geno * RING * PAIR + (x % RING) * PAIR + far % PAIR))
    return lax.ppermute(cells, BOTH, pairs)


def spread(cells, ring, pair, direct):
    side = hop(cells, **{pair: 1})
    up = hop(cells, **{ring: 1})
    down = hop(cells, **{ring: -1})
    across = hop(cells, **{ring: 2})
    side_up = hop(side, **{ring: 1})
    side_down = hop(side, **{ring: -1})
    side_across = hop(side, **{ring: 2}) if direct else hop(across, **{pair: 1})
    return [
        (0, 0, cells),
        (0, 1, side),
        (1, 0, up),
        (-1, 0, down),
        (1, 1, side_up),
        (-1, 1, side_down),
        (2, 0, across),
        (2, 1, side_across),
    ]


def gather_geno(cells, direct):
    geno = lax.axis_index("geno")
    y, z, core = geno // 4, geno // 2 % 2, geno % 2
    pieces, order = [], []
    for a, b, piece in spread(cells, "y", "z", direct):
        base = (((y - a) % RING) * PAIR + (z + b) % PAIR) * CORES
        pieces += [piece, hop(piece, core=1)]
        order += [base + core, base + 1 - core]
    return pieces, jnp.stack(order).astype(jnp.int32)


STRIP = 5


def split(values, count):
    terms = []
    for _ in range(count):
        terms.append(values.astype(BF16))
        values = values - terms[-1].astype(F32)
    return terms


def pack(core, trial, right, observed, coef, length, kernel_trial):
    rows, cols = right.shape
    count = kernel_trial.shape[1] // cols
    part, half = rows // count, kernel_trial.shape[0] // 2

    def body(core_ref, trial_ref, right_ref, seen_ref, coef_ref, length_ref, kernel_ref, slab_ref, strip_ref):
        below = pl.multiple_of(core_ref[0] * half, half)
        for r in range(STRIP):
            at = pl.multiple_of(lax.rem(trial_ref[0] + r, count) * cols, cols)
            block = kernel_ref[pl.ds(below, half), pl.ds(at, cols)]
            for t in range(count):
                strip_ref[t, r] = block
        line = lax.broadcasted_iota(jnp.int32, (16, cols), 0)
        extra = jnp.zeros((16, cols), F32)
        values = coef_ref[...]
        for k in range(3):
            term = values.astype(BF16).astype(F32)
            extra = jnp.where(line == k, term, extra)
            values = values - term
        extra = jnp.where(line == 3, length_ref[...].astype(F32), extra).astype(BF16)
        for t in range(count):
            at = slice(t * part, (t + 1) * part)
            high, low = split(right_ref[at], 2)
            slab_ref[t, :part] = high
            slab_ref[t, part : 2 * part] = low
            slab_ref[t, 2 * part : 3 * part] = seen_ref[at].astype(F32).astype(BF16)
            slab_ref[t, 3 * part :] = extra

    return pl.pallas_call(
        body,
        out_shape=[
            jax.ShapeDtypeStruct((count, 3 * part + 16, cols), BF16),
            jax.ShapeDtypeStruct((count, STRIP, half, cols), BF16),
        ],
        in_specs=[SMEM] * 2 + [VMEM] * 5,
        out_specs=[VMEM] * 2,
        compiler_params=pltpu.CompilerParams(vmem_limit_bytes=24 << 20),
    )(core, trial, right, observed, coef, length, kernel_trial)


def swap(slabs):
    return lax.all_to_all(slabs, "trial", split_axis=0, concat_axis=0, tiled=True)


def totals(row):
    devices = lax.axis_size("geno") * lax.axis_size("trial")
    copies = jnp.broadcast_to(row[None], (devices,) + row.shape)
    return jnp.sum(lax.all_to_all(copies, BOTH, 0, 0, tiled=True), axis=(0, 1))


def mix(kernel, pieces, order, kind):
    count = len(pieces)
    rows, cols = pieces[0].shape

    def body(order_ref, kernel_ref, *refs):
        out_ref, total = refs[count], refs[count + 1]
        for k in range(count):
            at = pl.ds(pl.multiple_of(order_ref[k] * rows, rows), rows)
            for m in range(0, rows, 256):
                term = jnp.dot(
                    kernel_ref[m : m + 256, at], refs[k][...], preferred_element_type=F32
                )
                if k == 0:
                    total[m : m + 256] = term
                elif k < count - 1:
                    total[m : m + 256] += term
                else:
                    out_ref[m : m + 256] = (total[m : m + 256] + term).astype(out_ref.dtype)

    return pl.pallas_call(
        body,
        out_shape=jax.ShapeDtypeStruct((rows, cols), kind),
        in_specs=[SMEM] + [VMEM] * (1 + count),
        out_specs=VMEM,
        scratch_shapes=[pltpu.VMEM((rows, cols), F32)],
        compiler_params=pltpu.CompilerParams(vmem_limit_bytes=32 << 20),
        cost_estimate=pl.CostEstimate(
            flops=2 * rows * rows * cols * count,
            bytes_accessed=(rows * rows + rows * cols) * 2 * count,
            transcendentals=0,
        ),
    )(order, kernel, *pieces)


def fetch(core_ref, strip_refs, held, sems):
    copies = []
    half = strip_refs[0].shape[2]
    for side, strip_ref in enumerate(strip_refs):
        here = core_ref[0] if side == 0 else 1 - core_ref[0]
        at = pl.ds(pl.multiple_of(here * half, half), half)
        for t in range(strip_ref.shape[0]):
            copies.append(
                pltpu.make_async_copy(strip_ref.at[t], held.at[t, :, at], sems.at[side, t])
            )
    for copy in copies:
        copy.start()
    return copies


def multiply(left_ref, copies, held, total):
    total[...] = jnp.zeros_like(total)
    count = left_ref.shape[0]
    for t in range(count):
        copies[t].wait()
        copies[count + t].wait()
        for r in range(STRIP):
            other = (t + r) % count
            block = held[t, r]
            total[other] += jnp.dot(left_ref[t], block, preferred_element_type=F32)
            if 0 < r < STRIP - 1:
                total[t] += lax.dot_general(
                    left_ref[other], block, (((1,), (1,)), ((), ())), preferred_element_type=F32
                )


def cross_call(body, operands, strips, shapes, scratch):
    count, part, cols = operands[-1].shape
    return pl.pallas_call(
        body,
        out_shape=shapes,
        in_specs=[SMEM if x.ndim == 1 else VMEM for x in operands] + [ANY] * 2,
        out_specs=[VMEM] * len(shapes),
        scratch_shapes=scratch
        + [
            pltpu.VMEM((count, part, cols), F32),
            pltpu.VMEM((count, STRIP, cols, cols), BF16),
            pltpu.SemaphoreType.DMA((2, count)),
        ],
        compiler_params=pltpu.CompilerParams(vmem_limit_bytes=32 << 20),
        cost_estimate=pl.CostEstimate(
            flops=2 * part * (count * cols) ** 2,
            bytes_accessed=2 * (count * cols) ** 2,
            transcendentals=0,
        ),
    )(*operands, *strips)


def cross_first(core, mixed, seen, field, right, strips):
    count, part, cols = right.shape

    def body(core_ref, mixed_ref, seen_ref, field_ref, right_ref, *refs):
        image_ref, sums_ref, total, held, sems = refs[2:]
        multiply(mixed_ref, fetch(core_ref, refs[:2], held, sems), held, total)
        sums = [jnp.zeros((part, cols), F32) for _ in range(3)]
        for t in range(count):
            image = seen_ref[t].astype(F32) * total[t] + field_ref[t]
            image_ref[t] = image
            right_t = right_ref[t]
            terms = (right_t * right_t, right_t * image, image * image)
            sums = [a + b for a, b in zip(sums, terms)]
        lane = lax.broadcasted_iota(jnp.int32, (1, 128), 1)
        row = jnp.zeros((1, 128), F32)
        for k in range(3):
            row = jnp.where(lane == k, jnp.sum(sums[k]), row)
        sums_ref[...] = row

    shapes = [jax.ShapeDtypeStruct(right.shape, F32), jax.ShapeDtypeStruct((1, 128), F32)]
    return cross_call(body, [core, mixed, seen, field, right], strips, shapes, [])


def cross_second(core, factors, seen, right, image, strips):
    count, part, cols = right.shape

    def body(core_ref, factor_ref, seen_ref, right_ref, image_ref, *refs):
        out_ref, left, total, held, sems = refs[2:]
        copies = fetch(core_ref, refs[:2], held, sems)
        for t in range(count):
            right_t = right_ref[t]
            direction = right_t - factor_ref[0] * image_ref[t] + factor_ref[1] * right_t
            high, low = split(image_ref[t], 2)
            out_ref[t, part : 2 * part] = high
            out_ref[t, 2 * part :] = low
            left[t] = (seen_ref[t].astype(F32) * direction).astype(BF16)
        multiply(left, copies, held, total)
        for t in range(count):
            out_ref[t, :part] = total[t].astype(BF16)

    shapes = [jax.ShapeDtypeStruct((count, 3 * part, cols), BF16)]
    return cross_call(
        body,
        [core, factors, seen, right, image],
        strips,
        shapes,
        [pltpu.VMEM(right.shape, BF16)],
    )[0]


def links_of(first, rows, row_length, total_rows):
    position = (first - 1 + lax.iota(jnp.int32, rows + 1))[:, None]
    length = row_length.astype(F32)
    later = (position + 1).astype(F32)
    whole_rows = jnp.floor((later + 0.5) / length) * length
    keep = (position >= 0) & (position + 1 < total_rows) & (later != whole_rows)
    return keep.astype(F32)


def field_of(cells, above, below, links, coef):
    padded = jnp.concatenate([above, cells, below], axis=-2)
    flux = links * (padded[..., 1:, :] - padded[..., :-1, :])
    return cells - coef * (flux[..., 1:, :] - flux[..., :-1, :])


def on_device(right_side, observed, row_length, field_coef, kernel_geno, kernel_trial):
    count = lax.axis_size("trial")
    rows, cols = observed.shape
    part = rows // count
    genos = lax.axis_size("geno")
    total_rows = rows * genos
    geno, trial = lax.axis_index("geno"), lax.axis_index("trial")
    right = right_side[:, 0, :]
    seen = observed.astype(F32)

    core = (geno % CORES).astype(jnp.int32)[None]
    pieces, order = gather_geno((seen * right).astype(BF16), True)
    slabs, strips = pack(
        core, trial[None], right, observed, field_coef[None], row_length[None], kernel_trial
    )
    slabs, strips, pieces[2] = lax.optimization_barrier((slabs, strips, pieces[2]))
    strips = swap(strips)
    strips = [strips, hop(strips, core=1)]
    slabs = swap(slabs)
    mixed = mix(kernel_geno, pieces, order, BF16)

    right_r = slabs[:, :part].astype(F32) + slabs[:, part : 2 * part].astype(F32)
    seen_r = slabs[:, 2 * part : 3 * part]
    extra = slabs[:, 3 * part :].astype(F32)
    coef_r = extra[:, 0:1] + extra[:, 1:2] + extra[:, 2:3]
    length_r = extra[:, 3:4]
    devices = count * genos
    above = lax.ppermute(right_r[:, -1:], BOTH, [(i, i + 1) for i in range(devices - 1)])
    below = lax.ppermute(right_r[:, :1], BOTH, [(i + 1, i) for i in range(devices - 1)])
    links_r = links_of(geno * rows + trial * part, part, length_r, total_rows)
    field_r = field_of(right_r, above, below, links_r, coef_r)

    mixed_r = swap(mixed.reshape(count, part, cols))
    image_r, sums = cross_first(core, mixed_r, seen_r, field_r, right_r, strips)
    sums = totals(sums)
    rr, ri, ii = sums[0], sums[1], sums[2]
    alpha = rr / ri
    new = rr - 2.0 * alpha * ri + alpha * alpha * ii
    beta = new / rr

    factors = jnp.stack([alpha, beta])
    turned = swap(cross_second(core, factors, seen_r, right_r, image_r, strips))
    pieces, order = gather_geno(turned[:, :part].reshape(rows, cols), False)
    crossed = mix(kernel_geno, pieces, order, F32)
    image = turned[:, part : 2 * part].astype(F32) + turned[:, 2 * part :].astype(F32)
    image = image.reshape(rows, cols)
    residual = right - alpha * image
    direction = residual + beta * right
    above = lax.ppermute(direction[-1:], "geno", [(i, i + 1) for i in range(genos - 1)])
    below = lax.ppermute(direction[:1], "geno", [(i + 1, i) for i in range(genos - 1)])
    links = links_of(geno * rows, rows, row_length[None], total_rows)
    field = field_of(direction, above, below, links, field_coef[None])
    image = seen * crossed + field
    product = jnp.zeros((1, 128), F32).at[0, 0].set(jnp.sum(direction * image))
    product = totals(product)[0]
    step = new / product
    solution_field = alpha * right + step * direction
    residual = residual - step * image
    return solution_field[:, None, :], residual[:, None, :]


def solution(mesh):
    return jax.shard_map(
        on_device,
        mesh=mesh,
        in_specs=(
            P("geno", None, "trial"),
            P("geno", "trial"),
            P("trial"),
            P("trial"),
            P("geno", None),
            P("trial", None),
        ),
        out_specs=(P("geno", None, "trial"), P("geno", None, "trial")),
        check_vma=False,
    )
```

```python
import jax
import jax.numpy as jnp
from jax import lax
from jax.experimental import pallas as pl
from jax.experimental.pallas import tpu as pltpu
from jax.sharding import PartitionSpec as P

BOTH = ("geno", "trial")
RING, PAIR, CORES = 4, 2, 2
F32, BF16 = jnp.float32, jnp.bfloat16
SMEM = pl.BlockSpec(memory_space=pltpu.SMEM)
VMEM = pl.BlockSpec(memory_space=pltpu.VMEM)
HBM = pl.BlockSpec(memory_space=pltpu.HBM)


def place(index):
    geno, trial = divmod(index, RING * PAIR)
    return (geno // 4, geno // 2 % 2, geno % 2, trial // 2, trial % 2)


def hop(cells, **by):
    step = [by.get(name, 0) for name in ("y", "z", "core", "x", "far")]
    pairs = []
    for index in range(RING * PAIR * CORES * RING * PAIR):
        y, z, core, x, far = (a + b for a, b in zip(place(index), step))
        geno = ((y % RING) * PAIR + z % PAIR) * CORES + core % CORES
        pairs.append((index, geno * RING * PAIR + (x % RING) * PAIR + far % PAIR))
    return lax.ppermute(cells, BOTH, pairs)


def together(*arrays):
    return lax.optimization_barrier(arrays)


STEPS = [(0, 0), (0, 1), (1, 0), (-1, 0), (2, 0), (1, 1), (-1, 1), (2, 1)]


def gather_geno(cells, kernel, *waiting, strip=None):
    geno = lax.axis_index("geno")
    y, z, core = geno // 4, geno // 2 % 2, geno % 2
    side, up = hop(cells, z=1), hop(cells, y=1)
    down, across = hop(cells, y=-1), hop(cells, y=2)
    strips, later = [], []
    if strip is not None:
        strips = [hop(strip, **{name: by}) for name, by in (("far", 1), ("x", 1), ("x", -1), ("x", 2))]
    side, up, down, across, kernel, *rest = together(
        side, up, down, across, kernel, *waiting, *strips
    )
    waiting, strips = rest[: len(waiting)], rest[len(waiting) :]
    if strip is not None:
        waiting = [swap(cells) for cells in waiting]
        later = [hop(strips[0], x=by) for by in (1, -1, 2)] + waiting
        side_across = hop(side, y=2)
    else:
        side_across = hop(across, z=1)
    side_up, side_down = hop(side, y=1), hop(side, y=-1)
    others = [hop(piece, core=1) for piece in (cells, side, up, down, across)]
    order = []
    for a, b in STEPS:
        base = (((y - a) % RING) * PAIR + (z + b) % PAIR) * CORES
        order += [base + core, base + 1 - core]
    order = jnp.stack(order).astype(jnp.int32)
    pieces = [cells, others[0], side, others[1], up, others[2], down, others[3], across, others[4]]
    carry = mix_part(kernel, pieces, order[:10], None, F32)
    carry, side_up, side_down, side_across, *later = together(
        carry, side_up, side_down, side_across, *later
    )
    pieces = []
    for piece in (side_up, side_down, side_across):
        pieces += [piece, hop(piece, core=1)]
    gathered = (kernel, pieces, order[10:], carry)
    if strip is None:
        return gathered, waiting
    return gathered, later[3:], [strip] + strips + later[:3]


STRIP = 5


def split(values, count):
    terms = []
    for _ in range(count):
        terms.append(values.astype(BF16))
        values = values - terms[-1].astype(F32)
    return terms


def strip_of(core, trial, kernel):
    half, width = kernel.shape[0] // 2, STRIP * kernel.shape[0]
    rows = lax.dynamic_slice_in_dim(kernel, core * half, half, axis=0)
    rows = jnp.concatenate([rows, rows[:, : width - kernel.shape[0]]], axis=1)
    return lax.dynamic_slice_in_dim(rows, trial * kernel.shape[0], width, axis=1)


def pack(count, right, observed, coef, length, above, below):
    rows, cols = right.shape
    part = rows // count

    def body(right_ref, seen_ref, coef_ref, length_ref, above_ref, below_ref, out_ref):
        line = lax.broadcasted_iota(jnp.int32, (16, cols), 0)

        def put(extra, first, values, terms):
            for k in range(terms):
                term = values.astype(BF16).astype(F32)
                extra = jnp.where(line == first + k, term, extra)
                values = values - term
            return extra

        common = put(jnp.zeros((16, cols), F32), 0, coef_ref[...], 3)
        common = put(common, 3, length_ref[...].astype(F32), 1)
        for t in range(count):
            first, last = t * part, (t + 1) * part
            before = right_ref[first - 1 : first] if t else above_ref[...]
            behind = right_ref[last : last + 1] if last < rows else below_ref[...]
            extra = put(put(common, 4, before, 2), 6, behind, 2)
            high, low = split(right_ref[first:last], 2)
            seen = seen_ref[first:last].astype(F32).astype(BF16)
            for k, piece in enumerate((high, low, seen, extra.astype(BF16))):
                out_ref[t, k * part : k * part + piece.shape[0]] = piece

    return pl.pallas_call(
        body,
        out_shape=jax.ShapeDtypeStruct((count, 3 * part + 16, cols), BF16),
        in_specs=[VMEM] * 6,
        out_specs=VMEM,
        compiler_params=pltpu.CompilerParams(vmem_limit_bytes=10 << 20),
    )(right, observed, coef, length, above, below)


def right_of(slab_ref, t, part):
    return slab_ref[t, :part].astype(F32) + slab_ref[t, part : 2 * part].astype(F32)


def seen_of(slab_ref, t, part):
    return slab_ref[t, 2 * part : 3 * part].astype(F32)


def swap(slabs):
    return lax.all_to_all(slabs, "trial", split_axis=0, concat_axis=0, tiled=True)


def exchange(rows):
    return lax.all_to_all(rows, BOTH, 0, 0, tiled=True)


def lanes(values):
    lane = lax.broadcasted_iota(jnp.int32, (1, 128), 1)
    row = jnp.zeros((1, 128), F32)
    for k, value in enumerate(values):
        row = jnp.where(lane == k, value, row)
    return row


def in_hbm(arrays):
    return [pltpu.with_memory_space_constraint(cells, pltpu.HBM) for cells in arrays]


def mix(kernel, pieces, order, finish, carry, others, shapes):
    count = len(pieces)
    rows, cols = pieces[0].shape
    others = ([] if carry is None else [carry]) + others

    def body(order_ref, kernel_ref, *refs):
        piece_refs, rest = refs[:count], refs[count:-4]
        blocks, cells, total, sems = refs[-4:]
        copies = []
        for k in range(count):
            at = pl.ds(pl.multiple_of(order_ref[k] * rows, rows), rows)
            copies.append(
                (
                    pltpu.make_async_copy(kernel_ref.at[:, at], blocks.at[k], sems.at[k, 0]),
                    pltpu.make_async_copy(piece_refs[k], cells.at[k], sems.at[k, 1]),
                )
            )
        for pair in copies:
            for copy in pair:
                copy.start()
        if carry is not None:
            total[...] = rest[0][...]
            rest = rest[1:]
        for k in range(count):
            for copy in copies[k]:
                copy.wait()
            for m in range(0, rows, 256):
                term = jnp.dot(blocks[k, m : m + 256], cells[k], preferred_element_type=F32)
                if carry is None and k == 0:
                    total[m : m + 256] = term
                else:
                    total[m : m + 256] += term
        finish(total, *rest)

    return pl.pallas_call(
        body,
        out_shape=shapes,
        in_specs=[SMEM] + [HBM] * (1 + count) + [VMEM] * len(others),
        out_specs=[VMEM] * len(shapes),
        scratch_shapes=[
            pltpu.VMEM((count, rows, rows), BF16),
            pltpu.VMEM((count, rows, cols), BF16),
            pltpu.VMEM((rows, cols), F32),
            pltpu.SemaphoreType.DMA((count, 2)),
        ],
        compiler_params=pltpu.CompilerParams(vmem_limit_bytes=26 << 20),
    )(order, *in_hbm([kernel, *pieces]), *others)


def mix_part(kernel, pieces, order, carry, kind):
    def finish(total, out_ref):
        out_ref[...] = total[...].astype(kind)

    shapes = [jax.ShapeDtypeStruct(pieces[0].shape, kind)]
    return mix(kernel, pieces, order, finish, carry, [], shapes)[0]


def mix_second(kernel, pieces, order, carry, seen, field, direction, devices):
    rows, cols = seen.shape

    def finish(total, seen_ref, field_ref, direction_ref, image_ref, sums_ref):
        part = 128
        product = jnp.zeros((8, cols), F32)
        for m in range(0, rows, part):
            at = slice(m, m + part)
            image = seen_ref[at].astype(F32) * total[at] + field_ref[at]
            image_ref[at] = image
            terms = direction_ref[at] * image
            product += jnp.sum(terms.reshape(part // 8, 8, cols), axis=0)
        sums_ref[...] = jnp.broadcast_to(lanes([jnp.sum(product)])[None], sums_ref.shape)

    shapes = [
        jax.ShapeDtypeStruct((rows, cols), F32),
        jax.ShapeDtypeStruct((devices, 1, 128), F32),
    ]
    return mix(kernel, pieces, order, finish, carry, [seen, field, direction], shapes)


def fetch(order_ref, strip_refs, held, sems):
    copies = []
    for k, strip_ref in enumerate(strip_refs):
        here = order_ref[8] if k % 2 == 0 else 1 - order_ref[8]
        target = held.at[k // 2, here]
        copies.append(pltpu.make_async_copy(strip_ref, target, sems.at[k // 2, k % 2]))
    for copy in copies:
        copy.start()
    return copies


def multiply(order_ref, left_ref, copies, held, total):
    total[...] = jnp.zeros_like(total)
    count = left_ref.shape[0]
    cols = held.shape[3] // STRIP
    for slot in range(count):
        for side in range(2):
            copies[2 * slot + side].wait()
        t = order_ref[slot]
        for r in range(STRIP):
            other = lax.rem(t + r, count)
            at = slice(r * cols, (r + 1) * cols)
            block = jnp.concatenate([held[slot, 0, :, at], held[slot, 1, :, at]], axis=0)
            total[other] += jnp.dot(left_ref[t], block, preferred_element_type=F32)
            if 0 < r < STRIP - 1:
                total[t] += lax.dot_general(
                    left_ref[other], block, (((1,), (1,)), ((), ())), preferred_element_type=F32
                )


def cross_call(body, size, operands, strips, shapes, scratch):
    count, part, cols = size
    return pl.pallas_call(
        body,
        out_shape=shapes,
        in_specs=[SMEM if x.ndim == 1 else VMEM for x in operands] + [HBM] * len(strips),
        out_specs=[VMEM] * len(shapes),
        scratch_shapes=scratch
        + [
            pltpu.VMEM((count, part, cols), F32),
            pltpu.VMEM((count, 2) + strips[0].shape, BF16),
            pltpu.SemaphoreType.DMA((count, 2)),
        ],
        compiler_params=pltpu.CompilerParams(vmem_limit_bytes=14 << 20),
        cost_estimate=pl.CostEstimate(
            flops=2 * part * (count * cols) ** 2,
            bytes_accessed=2 * (count * cols) ** 2,
            transcendentals=0,
        ),
    )(*operands, *in_hbm(strips))


def cross_first(order, mixed, slabs, strips, total_rows, devices):
    count, part, cols = mixed.shape

    def body(order_ref, mixed_ref, slab_ref, *refs):
        image_ref, sums_ref, total, held, sems = refs[16:]
        multiply(order_ref, mixed_ref, fetch(order_ref, refs[:16], held, sems), held, total)
        sums = [jnp.zeros((part, cols), F32) for _ in range(3)]
        line = lax.broadcasted_iota(jnp.int32, (part, cols), 0)
        first = order_ref[9]
        for t in range(count):
            right = right_of(slab_ref, t, part)
            extra = slab_ref[t, 3 * part :].astype(F32)
            coef = extra[0:1] + extra[1:2] + extra[2:3]
            length = extra[3:4]
            above = jnp.where(line == 0, extra[4:5] + extra[5:6], pltpu.roll(right, 1, 0))
            below = jnp.where(
                line == part - 1, extra[6:7] + extra[7:8], pltpu.roll(right, part - 1, 0)
            )
            flux = linked(first + line, length, total_rows) * (below - right)
            flux -= linked(first + line - 1, length, total_rows) * (right - above)
            image = seen_of(slab_ref, t, part) * total[t] + (right - coef * flux)
            image_ref[t] = image
            terms = (right * right, right * image, image * image)
            sums = [a + b for a, b in zip(sums, terms)]
        row = lanes([jnp.sum(total) for total in sums])
        sums_ref[...] = jnp.broadcast_to(row[None], sums_ref.shape)

    shapes = [
        jax.ShapeDtypeStruct(mixed.shape, F32),
        jax.ShapeDtypeStruct((devices, 1, 128), F32),
    ]
    return cross_call(body, mixed.shape, [order, mixed, slabs], strips, shapes, [])


def cross_second(order, sums, slabs, image, strips):
    count, part, cols = image.shape

    def body(order_ref, sums_ref, slab_ref, image_ref, *refs):
        out_ref, factor_ref, left, total, held, sems = refs[16:]
        copies = fetch(order_ref, refs[:16], held, sems)
        sums = jnp.sum(sums_ref[...], axis=0)
        rr, ri, ii = sums[:, 0:1], sums[:, 1:2], sums[:, 2:3]
        alpha = rr / ri
        new = rr - 2.0 * alpha * ri + alpha * alpha * ii
        beta = new / rr
        factor_ref[...] = lanes([alpha, beta, new])
        for t in range(count):
            right = right_of(slab_ref, t, part)
            direction = right - alpha * image_ref[t] + beta * right
            high, low = split(image_ref[t], 2)
            out_ref[t, part : 2 * part] = high
            out_ref[t, 2 * part :] = low
            left[t] = (seen_of(slab_ref, t, part) * direction).astype(BF16)
        multiply(order_ref, left, copies, held, total)
        for t in range(count):
            out_ref[t, :part] = total[t].astype(BF16)

    shapes = [
        jax.ShapeDtypeStruct((count, 3 * part, cols), BF16),
        jax.ShapeDtypeStruct((1, 128), F32),
    ]
    scratch = [pltpu.VMEM(image.shape, BF16)]
    return cross_call(body, image.shape, [order, sums, slabs, image], strips, shapes, scratch)


def conclude(sums, factors, right, direction, residual, image):
    rows, cols = right.shape

    def body(sums_ref, factor_ref, right_ref, direction_ref, residual_ref, image_ref, *outs):
        product = jnp.sum(sums_ref[...], axis=0)[:, 0:1]
        alpha, new = factor_ref[:, 0:1], factor_ref[:, 2:3]
        step = new / product
        part = 128
        for m in range(0, rows, part):
            at = slice(m, m + part)
            field = alpha * right_ref[at] + step * direction_ref[at]
            outs[0][at] = field[:, None, :]
            outs[1][at] = (residual_ref[at] - step * image_ref[at])[:, None, :]

    return pl.pallas_call(
        body,
        out_shape=[jax.ShapeDtypeStruct((rows, 1, cols), F32)] * 2,
        in_specs=[VMEM] * 6,
        out_specs=[VMEM] * 2,
        compiler_params=pltpu.CompilerParams(vmem_limit_bytes=10 << 20),
    )(sums, factors, right, direction, residual, image)


def linked(position, length, total_rows):
    later = (position + 1).astype(F32)
    whole_rows = jnp.floor((later + 0.5) / length) * length
    keep = (position >= 0) & (position + 1 < total_rows) & (later != whole_rows)
    return jnp.where(keep, 1.0, 0.0)


def field_of(cells, above, below, links, coef):
    padded = jnp.concatenate([above, cells, below], axis=-2)
    flux = links * (padded[..., 1:, :] - padded[..., :-1, :])
    return cells - coef * (flux[..., 1:, :] - flux[..., :-1, :])


def on_device(right_side, observed, row_length, field_coef, kernel_geno, kernel_trial):
    count = lax.axis_size("trial")
    rows, cols = observed.shape
    part = rows // count
    genos = lax.axis_size("geno")
    total_rows = rows * genos
    geno, trial = lax.axis_index("geno"), lax.axis_index("trial")
    right = right_side[:, 0, :]
    seen = observed.astype(F32)

    core = geno % CORES
    devices = count * genos
    following = [(i, i + 1) for i in range(genos - 1)]
    previous = [(i + 1, i) for i in range(genos - 1)]
    above = lax.ppermute(right[-1:], "geno", following)
    below = lax.ppermute(right[:1], "geno", previous)
    slabs = pack(count, right, observed, field_coef[None], row_length[None], above, below)
    strip = strip_of(core, trial, kernel_trial)
    gathered, (slabs,), strips = gather_geno(
        (seen * right).astype(BF16), kernel_geno, slabs, strip=strip
    )
    mixed = mix_part(*gathered, BF16)
    mixed, *strips = together(mixed, *strips)
    mixed_r = swap(mixed.reshape(count, part, cols))
    strips = [piece for own in strips for piece in (own, hop(own, core=1))]
    x, far = trial // PAIR, trial % PAIR
    order = [((x - a) % RING) * PAIR + (far + b) % PAIR for a, b in STEPS]
    order = jnp.stack(order + [core, geno * rows + trial * part]).astype(jnp.int32)

    image_r, sums = cross_first(order, mixed_r, slabs, strips, total_rows, devices)
    turned, factors = cross_second(order, exchange(sums), slabs, image_r, strips)
    turned = swap(turned)
    gathered, (turned,) = gather_geno(
        turned[:, :part].reshape(rows, cols), kernel_geno, turned
    )

    alpha, beta, new = factors[:, 0:1], factors[:, 1:2], factors[:, 2:3]
    image = turned[:, part : 2 * part].astype(F32) + turned[:, 2 * part :].astype(F32)
    image = image.reshape(rows, cols)
    residual = right - alpha * image
    direction = residual + beta * right
    above = lax.ppermute(direction[-1:], "geno", following)
    below = lax.ppermute(direction[:1], "geno", previous)
    position = (geno * rows - 1 + lax.iota(jnp.int32, rows + 1))[:, None]
    links = linked(position, row_length[None].astype(F32), total_rows)
    field = field_of(direction, above, below, links, field_coef[None])
    image, sums = mix_second(*gathered, seen.astype(BF16), field, direction, devices)
    return conclude(exchange(sums), factors, right, direction, residual, image)


def solution(mesh):
    return jax.shard_map(
        on_device,
        mesh=mesh,
        in_specs=(
            P("geno", None, "trial"),
            P("geno", "trial"),
            P("trial"),
            P("trial"),
            P("geno", None),
            P("trial", None),
        ),
        out_specs=(P("geno", None, "trial"), P("geno", None, "trial")),
        check_vma=False,
    )
```

```python
import jax
import jax.numpy as jnp
from jax import lax
from jax.experimental import pallas as pl
from jax.experimental.pallas import tpu as pltpu
from jax.sharding import PartitionSpec as P

BOTH = ("geno", "trial")
RING, PAIR, CORES = 4, 2, 2
F32, BF16 = jnp.float32, jnp.bfloat16
SMEM = pl.BlockSpec(memory_space=pltpu.SMEM)
VMEM = pl.BlockSpec(memory_space=pltpu.VMEM)
HBM = pl.BlockSpec(memory_space=pltpu.HBM)


def place(index):
    geno, trial = divmod(index, RING * PAIR)
    return (geno // 4, geno // 2 % 2, geno % 2, trial // 2, trial % 2)


def hop(cells, **by):
    step = [by.get(name, 0) for name in ("y", "z", "core", "x", "far")]
    pairs = []
    for index in range(RING * PAIR * CORES * RING * PAIR):
        y, z, core, x, far = (a + b for a, b in zip(place(index), step))
        geno = ((y % RING) * PAIR + z % PAIR) * CORES + core % CORES
        pairs.append((index, geno * RING * PAIR + (x % RING) * PAIR + far % PAIR))
    return lax.ppermute(cells, BOTH, pairs)


def together(*arrays):
    return lax.optimization_barrier(arrays)


STEPS = [(0, 0), (0, 1), (1, 0), (-1, 0), (2, 0), (1, 1), (-1, 1), (2, 1)]


def gather_geno(cells, kernel, *waiting, spread=False):
    geno = lax.axis_index("geno")
    y, z, core = geno // 4, geno // 2 % 2, geno % 2
    side, up = hop(cells, z=1), hop(cells, y=1)
    down, across = hop(cells, y=-1), hop(cells, y=2)
    side, up, down, across, kernel, *waiting = together(side, up, down, across, kernel, *waiting)
    if spread:
        waiting = [swap(cells) for cells in waiting]
        side_across = hop(side, y=2)
    else:
        side_across = hop(across, z=1)
    side_up, side_down = hop(side, y=1), hop(side, y=-1)
    others = [hop(piece, core=1) for piece in (cells, side, up, down, across)]
    order = []
    for a, b in STEPS:
        base = (((y - a) % RING) * PAIR + (z + b) % PAIR) * CORES
        order += [base + core, base + 1 - core]
    order = jnp.stack(order).astype(jnp.int32)
    pieces = [cells, others[0], side, others[1], up, others[2], down, others[3], across, others[4]]
    carry = mix_part(kernel, pieces, order[:10], None, F32)
    carry, side_up, side_down, side_across = together(carry, side_up, side_down, side_across)
    pieces = []
    for piece in (side_up, side_down, side_across):
        pieces += [piece, hop(piece, core=1)]
    if spread:
        pieces[0], *waiting = together(pieces[0], *waiting)
    return (kernel, pieces, order[10:], carry), waiting


STRIP = 5


def split(values, count):
    terms = []
    for _ in range(count):
        terms.append(values.astype(BF16))
        values = values - terms[-1].astype(F32)
    return terms


def strip_of(core, trial, kernel):
    half, width = kernel.shape[0] // 2, STRIP * kernel.shape[0]
    rows = lax.dynamic_slice_in_dim(kernel, core * half, half, axis=0)
    rows = jnp.concatenate([rows, rows[:, : width - kernel.shape[0]]], axis=1)
    return lax.dynamic_slice_in_dim(rows, trial * kernel.shape[0], width, axis=1)


def pack(count, right, observed, coef, length, above, below):
    rows, cols = right.shape
    part = rows // count

    def body(right_ref, seen_ref, coef_ref, length_ref, above_ref, below_ref, out_ref):
        line = lax.broadcasted_iota(jnp.int32, (16, cols), 0)

        def put(extra, first, values, terms):
            for k in range(terms):
                term = values.astype(BF16).astype(F32)
                extra = jnp.where(line == first + k, term, extra)
                values = values - term
            return extra

        common = put(jnp.zeros((16, cols), F32), 0, coef_ref[...], 3)
        common = put(common, 3, length_ref[...].astype(F32), 1)
        for t in range(count):
            first, last = t * part, (t + 1) * part
            before = right_ref[first - 1 : first] if t else above_ref[...]
            behind = right_ref[last : last + 1] if last < rows else below_ref[...]
            extra = put(put(common, 4, before, 2), 6, behind, 2)
            high, low = split(right_ref[first:last], 2)
            seen = seen_ref[first:last].astype(F32).astype(BF16)
            for k, piece in enumerate((high, low, seen, extra.astype(BF16))):
                out_ref[t, k * part : k * part + piece.shape[0]] = piece

    return pl.pallas_call(
        body,
        out_shape=jax.ShapeDtypeStruct((count, 3 * part + 16, cols), BF16),
        in_specs=[VMEM] * 6,
        out_specs=VMEM,
        compiler_params=pltpu.CompilerParams(vmem_limit_bytes=10 << 20),
    )(right, observed, coef, length, above, below)


def right_of(slab_ref, t, part):
    return slab_ref[t, :part].astype(F32) + slab_ref[t, part : 2 * part].astype(F32)


def seen_of(slab_ref, t, part):
    return slab_ref[t, 2 * part : 3 * part].astype(F32)


def swap(slabs):
    return lax.all_to_all(slabs, "trial", split_axis=0, concat_axis=0, tiled=True)


def exchange(rows):
    return lax.all_to_all(rows, BOTH, 0, 0, tiled=True)


def lanes(values):
    lane = lax.broadcasted_iota(jnp.int32, (1, 128), 1)
    row = jnp.zeros((1, 128), F32)
    for k, value in enumerate(values):
        row = jnp.where(lane == k, value, row)
    return row


def in_hbm(arrays):
    return [pltpu.with_memory_space_constraint(cells, pltpu.HBM) for cells in arrays]


def mix(kernel, pieces, order, finish, carry, others, shapes):
    count = len(pieces)
    rows, cols = pieces[0].shape
    others = ([] if carry is None else [carry]) + others

    def body(order_ref, kernel_ref, *refs):
        piece_refs, rest = refs[:count], refs[count:-4]
        blocks, cells, total, sems = refs[-4:]
        copies = []
        for k in range(count):
            at = pl.ds(pl.multiple_of(order_ref[k] * rows, rows), rows)
            copies.append(
                (
                    pltpu.make_async_copy(kernel_ref.at[:, at], blocks.at[k], sems.at[k, 0]),
                    pltpu.make_async_copy(piece_refs[k], cells.at[k], sems.at[k, 1]),
                )
            )
        for pair in copies:
            for copy in pair:
                copy.start()
        if carry is not None:
            total[...] = rest[0][...]
            rest = rest[1:]
        for k in range(count):
            for copy in copies[k]:
                copy.wait()
            for m in range(0, rows, 256):
                term = jnp.dot(blocks[k, m : m + 256], cells[k], preferred_element_type=F32)
                if carry is None and k == 0:
                    total[m : m + 256] = term
                else:
                    total[m : m + 256] += term
        finish(total, *rest)

    return pl.pallas_call(
        body,
        out_shape=shapes,
        in_specs=[SMEM] + [HBM] * (1 + count) + [VMEM] * len(others),
        out_specs=[VMEM] * len(shapes),
        scratch_shapes=[
            pltpu.VMEM((count, rows, rows), BF16),
            pltpu.VMEM((count, rows, cols), BF16),
            pltpu.VMEM((rows, cols), F32),
            pltpu.SemaphoreType.DMA((count, 2)),
        ],
        compiler_params=pltpu.CompilerParams(vmem_limit_bytes=26 << 20),
    )(order, *in_hbm([kernel, *pieces]), *others)


def mix_part(kernel, pieces, order, carry, kind):
    def finish(total, out_ref):
        out_ref[...] = total[...].astype(kind)

    shapes = [jax.ShapeDtypeStruct(pieces[0].shape, kind)]
    return mix(kernel, pieces, order, finish, carry, [], shapes)[0]


def mix_second(kernel, pieces, order, carry, seen, field, direction, devices):
    rows, cols = seen.shape

    def finish(total, seen_ref, field_ref, direction_ref, image_ref, sums_ref):
        part = 128
        product = jnp.zeros((8, cols), F32)
        for m in range(0, rows, part):
            at = slice(m, m + part)
            image = seen_ref[at].astype(F32) * total[at] + field_ref[at]
            image_ref[at] = image
            terms = direction_ref[at] * image
            product += jnp.sum(terms.reshape(part // 8, 8, cols), axis=0)
        sums_ref[...] = jnp.broadcast_to(lanes([jnp.sum(product)])[None], sums_ref.shape)

    shapes = [
        jax.ShapeDtypeStruct((rows, cols), F32),
        jax.ShapeDtypeStruct((devices, 1, 128), F32),
    ]
    return mix(kernel, pieces, order, finish, carry, [seen, field, direction], shapes)


def fetch(order_ref, strip_refs, held, sems):
    copies = []
    for t in range(held.shape[0]):
        for side, strip_ref in enumerate(strip_refs):
            here = order_ref[0] if side == 0 else 1 - order_ref[0]
            target = held.at[t, here]
            copies.append(pltpu.make_async_copy(strip_ref.at[t], target, sems.at[t, side]))
    for copy in copies:
        copy.start()
    return copies


def multiply(left_ref, copies, held, total):
    total[...] = jnp.zeros_like(total)
    count = left_ref.shape[0]
    cols = held.shape[3] // STRIP
    for t in range(count):
        for side in range(2):
            copies[2 * t + side].wait()
        for r in range(STRIP):
            other = (t + r) % count
            at = slice(r * cols, (r + 1) * cols)
            block = jnp.concatenate([held[t, 0, :, at], held[t, 1, :, at]], axis=0)
            total[other] += jnp.dot(left_ref[t], block, preferred_element_type=F32)
            if 0 < r < STRIP - 1:
                total[t] += lax.dot_general(
                    left_ref[other], block, (((1,), (1,)), ((), ())), preferred_element_type=F32
                )


def cross_call(body, size, operands, strips, shapes, scratch):
    count, part, cols = size
    return pl.pallas_call(
        body,
        out_shape=shapes,
        in_specs=[SMEM if x.ndim == 1 else VMEM for x in operands] + [HBM] * len(strips),
        out_specs=[VMEM] * len(shapes),
        scratch_shapes=scratch
        + [
            pltpu.VMEM((count, part, cols), F32),
            pltpu.VMEM((count, 2) + strips[0].shape[1:], BF16),
            pltpu.SemaphoreType.DMA((count, 2)),
        ],
        compiler_params=pltpu.CompilerParams(vmem_limit_bytes=14 << 20),
        cost_estimate=pl.CostEstimate(
            flops=2 * part * (count * cols) ** 2,
            bytes_accessed=2 * (count * cols) ** 2,
            transcendentals=0,
        ),
    )(*operands, *in_hbm(strips))


def cross_first(order, mixed, slabs, strips, total_rows, devices):
    count, part, cols = mixed.shape

    def body(order_ref, mixed_ref, slab_ref, *refs):
        image_ref, sums_ref, total, held, sems = refs[2:]
        multiply(mixed_ref, fetch(order_ref, refs[:2], held, sems), held, total)
        sums = [jnp.zeros((part, cols), F32) for _ in range(3)]
        line = lax.broadcasted_iota(jnp.int32, (part, cols), 0)
        first = order_ref[1]
        for t in range(count):
            right = right_of(slab_ref, t, part)
            extra = slab_ref[t, 3 * part :].astype(F32)
            coef = extra[0:1] + extra[1:2] + extra[2:3]
            length = extra[3:4]
            above = jnp.where(line == 0, extra[4:5] + extra[5:6], pltpu.roll(right, 1, 0))
            below = jnp.where(
                line == part - 1, extra[6:7] + extra[7:8], pltpu.roll(right, part - 1, 0)
            )
            flux = linked(first + line, length, total_rows) * (below - right)
            flux -= linked(first + line - 1, length, total_rows) * (right - above)
            image = seen_of(slab_ref, t, part) * total[t] + (right - coef * flux)
            image_ref[t] = image
            terms = (right * right, right * image, image * image)
            sums = [a + b for a, b in zip(sums, terms)]
        row = lanes([jnp.sum(total) for total in sums])
        sums_ref[...] = jnp.broadcast_to(row[None], sums_ref.shape)

    shapes = [
        jax.ShapeDtypeStruct(mixed.shape, F32),
        jax.ShapeDtypeStruct((devices, 1, 128), F32),
    ]
    return cross_call(body, mixed.shape, [order, mixed, slabs], strips, shapes, [])


def cross_second(order, sums, slabs, image, strips):
    count, part, cols = image.shape

    def body(order_ref, sums_ref, slab_ref, image_ref, *refs):
        out_ref, factor_ref, left, total, held, sems = refs[2:]
        copies = fetch(order_ref, refs[:2], held, sems)
        sums = jnp.sum(sums_ref[...], axis=0)
        rr, ri, ii = sums[:, 0:1], sums[:, 1:2], sums[:, 2:3]
        alpha = rr / ri
        new = rr - 2.0 * alpha * ri + alpha * alpha * ii
        beta = new / rr
        factor_ref[...] = lanes([alpha, beta, new])
        for t in range(count):
            right = right_of(slab_ref, t, part)
            direction = right - alpha * image_ref[t] + beta * right
            high, low = split(image_ref[t], 2)
            out_ref[t, part : 2 * part] = high
            out_ref[t, 2 * part :] = low
            left[t] = (seen_of(slab_ref, t, part) * direction).astype(BF16)
        multiply(left, copies, held, total)
        for t in range(count):
            out_ref[t, :part] = total[t].astype(BF16)

    shapes = [
        jax.ShapeDtypeStruct((count, 3 * part, cols), BF16),
        jax.ShapeDtypeStruct((1, 128), F32),
    ]
    scratch = [pltpu.VMEM(image.shape, BF16)]
    return cross_call(body, image.shape, [order, sums, slabs, image], strips, shapes, scratch)


def conclude(sums, factors, right, direction, residual, image):
    rows, cols = right.shape

    def body(sums_ref, factor_ref, right_ref, direction_ref, residual_ref, image_ref, *outs):
        product = jnp.sum(sums_ref[...], axis=0)[:, 0:1]
        alpha, new = factor_ref[:, 0:1], factor_ref[:, 2:3]
        step = new / product
        part = 128
        for m in range(0, rows, part):
            at = slice(m, m + part)
            field = alpha * right_ref[at] + step * direction_ref[at]
            outs[0][at] = field[:, None, :]
            outs[1][at] = (residual_ref[at] - step * image_ref[at])[:, None, :]

    return pl.pallas_call(
        body,
        out_shape=[jax.ShapeDtypeStruct((rows, 1, cols), F32)] * 2,
        in_specs=[VMEM] * 6,
        out_specs=[VMEM] * 2,
        compiler_params=pltpu.CompilerParams(vmem_limit_bytes=10 << 20),
    )(sums, factors, right, direction, residual, image)


def linked(position, length, total_rows):
    later = (position + 1).astype(F32)
    whole_rows = jnp.floor((later + 0.5) / length) * length
    keep = (position >= 0) & (position + 1 < total_rows) & (later != whole_rows)
    return jnp.where(keep, 1.0, 0.0)


def field_of(cells, above, below, links, coef):
    padded = jnp.concatenate([above, cells, below], axis=-2)
    flux = links * (padded[..., 1:, :] - padded[..., :-1, :])
    return cells - coef * (flux[..., 1:, :] - flux[..., :-1, :])


def on_device(right_side, observed, row_length, field_coef, kernel_geno, kernel_trial):
    count = lax.axis_size("trial")
    rows, cols = observed.shape
    part = rows // count
    genos = lax.axis_size("geno")
    total_rows = rows * genos
    geno, trial = lax.axis_index("geno"), lax.axis_index("trial")
    right = right_side[:, 0, :]
    seen = observed.astype(F32)

    core = geno % CORES
    devices = count * genos
    following = [(i, i + 1) for i in range(genos - 1)]
    previous = [(i + 1, i) for i in range(genos - 1)]
    above = lax.ppermute(right[-1:], "geno", following)
    below = lax.ppermute(right[:1], "geno", previous)
    slabs = pack(count, right, observed, field_coef[None], row_length[None], above, below)
    strip = strip_of(core, trial, kernel_trial)
    strips = lax.all_gather(strip, "trial", axis=0)
    gathered, (slabs,) = gather_geno(
        (seen * right).astype(BF16), kernel_geno, slabs, spread=True
    )
    mixed, strips = together(mix_part(*gathered, BF16), strips)
    mixed_r = swap(mixed.reshape(count, part, cols))
    strips = [strips, hop(strips, core=1)]
    order = jnp.stack([core, geno * rows + trial * part]).astype(jnp.int32)

    image_r, sums = cross_first(order, mixed_r, slabs, strips, total_rows, devices)
    turned, factors = cross_second(order, exchange(sums), slabs, image_r, strips)
    turned = swap(turned)
    gathered, (turned,) = gather_geno(
        turned[:, :part].reshape(rows, cols), kernel_geno, turned
    )

    alpha, beta, new = factors[:, 0:1], factors[:, 1:2], factors[:, 2:3]
    image = turned[:, part : 2 * part].astype(F32) + turned[:, 2 * part :].astype(F32)
    image = image.reshape(rows, cols)
    residual = right - alpha * image
    direction = residual + beta * right
    above = lax.ppermute(direction[-1:], "geno", following)
    below = lax.ppermute(direction[:1], "geno", previous)
    position = (geno * rows - 1 + lax.iota(jnp.int32, rows + 1))[:, None]
    links = linked(position, row_length[None].astype(F32), total_rows)
    field = field_of(direction, above, below, links, field_coef[None])
    image, sums = mix_second(*gathered, seen.astype(BF16), field, direction, devices)
    return conclude(exchange(sums), factors, right, direction, residual, image)


def solution(mesh):
    return jax.shard_map(
        on_device,
        mesh=mesh,
        in_specs=(
            P("geno", None, "trial"),
            P("geno", "trial"),
            P("trial"),
            P("trial"),
            P("geno", None),
            P("trial", None),
        ),
        out_specs=(P("geno", None, "trial"), P("geno", None, "trial")),
        check_vma=False,
    )
```

```python
import jax
import jax.numpy as jnp
from jax import lax
from jax.experimental import pallas as pl
from jax.experimental.pallas import tpu as pltpu
from jax.sharding import PartitionSpec as P

BOTH = ("geno", "trial")
RING, PAIR, CORES = 4, 2, 2
F32, BF16 = jnp.float32, jnp.bfloat16
SMEM = pl.BlockSpec(memory_space=pltpu.SMEM)
VMEM = pl.BlockSpec(memory_space=pltpu.VMEM)
HBM = pl.BlockSpec(memory_space=pltpu.HBM)


def place(index):
    geno, trial = divmod(index, RING * PAIR)
    return (geno // 4, geno // 2 % 2, geno % 2, trial // 2, trial % 2)


def hop(cells, **by):
    step = [by.get(name, 0) for name in ("y", "z", "core", "x", "far")]
    pairs = []
    for index in range(RING * PAIR * CORES * RING * PAIR):
        y, z, core, x, far = (a + b for a, b in zip(place(index), step))
        geno = ((y % RING) * PAIR + z % PAIR) * CORES + core % CORES
        pairs.append((index, geno * RING * PAIR + (x % RING) * PAIR + far % PAIR))
    return lax.ppermute(cells, BOTH, pairs)


def together(*arrays):
    return lax.optimization_barrier(arrays)


STEPS = [(0, 0), (0, 1), (1, 0), (-1, 0), (2, 0), (1, 1), (-1, 1), (2, 1)]


def gather_geno(cells, kernel, *waiting, spread=False):
    geno = lax.axis_index("geno")
    y, z, core = geno // 4, geno // 2 % 2, geno % 2
    side, up = hop(cells, z=1), hop(cells, y=1)
    down, across = hop(cells, y=-1), hop(cells, y=2)
    side, up, down, across, kernel, *waiting = together(side, up, down, across, kernel, *waiting)
    if spread:
        waiting = [swap(cells) for cells in waiting]
        side_across = hop(side, y=2)
    else:
        side_across = hop(across, z=1)
    side_up, side_down = hop(side, y=1), hop(side, y=-1)
    others = [hop(piece, core=1) for piece in (cells, side, up, down, across)]
    order = []
    for a, b in STEPS:
        base = (((y - a) % RING) * PAIR + (z + b) % PAIR) * CORES
        order += [base + core, base + 1 - core]
    order = jnp.stack(order).astype(jnp.int32)
    pieces = [cells, others[0], side, others[1], up, others[2], down, others[3], across, others[4]]
    carry = mix_part(kernel, pieces, order[:10], None, F32)
    if not spread:
        carry, *waiting = together(carry, *waiting)
    carry, side_up, side_down, side_across = together(carry, side_up, side_down, side_across)
    pieces = []
    for piece in (side_up, side_down, side_across):
        pieces += [piece, hop(piece, core=1)]
    if spread:
        pieces[0], *waiting = together(pieces[0], *waiting)
    return (kernel, pieces, order[10:], carry), waiting


STRIP = 5


def split(values, count):
    terms = []
    for _ in range(count):
        terms.append(values.astype(BF16))
        values = values - terms[-1].astype(F32)
    return terms


def strip_of(core, trial, kernel):
    half, width = kernel.shape[0] // 2, STRIP * kernel.shape[0]
    rows = lax.dynamic_slice_in_dim(kernel, core * half, half, axis=0)
    rows = jnp.concatenate([rows, rows[:, : width - kernel.shape[0]]], axis=1)
    return lax.dynamic_slice_in_dim(rows, trial * kernel.shape[0], width, axis=1)


def pack(count, right, observed, coef, length, above, below):
    rows, cols = right.shape
    part = rows // count

    def body(right_ref, seen_ref, coef_ref, length_ref, above_ref, below_ref, out_ref):
        line = lax.broadcasted_iota(jnp.int32, (16, cols), 0)

        def put(extra, first, values, terms):
            for k in range(terms):
                term = values.astype(BF16).astype(F32)
                extra = jnp.where(line == first + k, term, extra)
                values = values - term
            return extra

        common = put(jnp.zeros((16, cols), F32), 0, coef_ref[...], 3)
        common = put(common, 3, length_ref[...].astype(F32), 1)
        for t in range(count):
            first, last = t * part, (t + 1) * part
            before = right_ref[first - 1 : first] if t else above_ref[...]
            behind = right_ref[last : last + 1] if last < rows else below_ref[...]
            extra = put(put(common, 4, before, 2), 6, behind, 2)
            high, low = split(right_ref[first:last], 2)
            seen = seen_ref[first:last].astype(F32).astype(BF16)
            for k, piece in enumerate((high, low, seen, extra.astype(BF16))):
                out_ref[t, k * part : k * part + piece.shape[0]] = piece

    return pl.pallas_call(
        body,
        out_shape=jax.ShapeDtypeStruct((count, 3 * part + 16, cols), BF16),
        in_specs=[VMEM] * 6,
        out_specs=VMEM,
        compiler_params=pltpu.CompilerParams(vmem_limit_bytes=10 << 20),
    )(right, observed, coef, length, above, below)


def right_of(slab_ref, t, part):
    return slab_ref[t, :part].astype(F32) + slab_ref[t, part : 2 * part].astype(F32)


def seen_of(slab_ref, t, part):
    return slab_ref[t, 2 * part : 3 * part].astype(F32)


def swap(slabs):
    return lax.all_to_all(slabs, "trial", split_axis=0, concat_axis=0, tiled=True)


def exchange(rows):
    return lax.all_to_all(rows, BOTH, 0, 0, tiled=True)


def lanes(values):
    lane = lax.broadcasted_iota(jnp.int32, (1, 128), 1)
    row = jnp.zeros((1, 128), F32)
    for k, value in enumerate(values):
        row = jnp.where(lane == k, value, row)
    return row


def in_hbm(arrays):
    return [pltpu.with_memory_space_constraint(cells, pltpu.HBM) for cells in arrays]


def mix(kernel, pieces, order, finish, carry, others, shapes):
    count = len(pieces)
    rows, cols = pieces[0].shape
    others = ([] if carry is None else [carry]) + others

    def body(order_ref, kernel_ref, *refs):
        piece_refs, rest = refs[:count], refs[count:-4]
        blocks, cells, total, sems = refs[-4:]
        copies = []
        for k in range(count):
            at = pl.ds(pl.multiple_of(order_ref[k] * rows, rows), rows)
            copies.append(
                (
                    pltpu.make_async_copy(kernel_ref.at[:, at], blocks.at[k], sems.at[k, 0]),
                    pltpu.make_async_copy(piece_refs[k], cells.at[k], sems.at[k, 1]),
                )
            )
        for pair in copies:
            for copy in pair:
                copy.start()
        if carry is not None:
            total[...] = rest[0][...]
            rest = rest[1:]
        for k in range(count):
            for copy in copies[k]:
                copy.wait()
            for m in range(0, rows, 256):
                term = jnp.dot(blocks[k, m : m + 256], cells[k], preferred_element_type=F32)
                if carry is None and k == 0:
                    total[m : m + 256] = term
                else:
                    total[m : m + 256] += term
        finish(total, *rest)

    return pl.pallas_call(
        body,
        out_shape=shapes,
        in_specs=[SMEM] + [HBM] * (1 + count) + [VMEM] * len(others),
        out_specs=[VMEM] * len(shapes),
        scratch_shapes=[
            pltpu.VMEM((count, rows, rows), BF16),
            pltpu.VMEM((count, rows, cols), BF16),
            pltpu.VMEM((rows, cols), F32),
            pltpu.SemaphoreType.DMA((count, 2)),
        ],
        compiler_params=pltpu.CompilerParams(vmem_limit_bytes=26 << 20),
    )(order, *in_hbm([kernel, *pieces]), *others)


def mix_part(kernel, pieces, order, carry, kind):
    def finish(total, out_ref):
        out_ref[...] = total[...].astype(kind)

    shapes = [jax.ShapeDtypeStruct(pieces[0].shape, kind)]
    return mix(kernel, pieces, order, finish, carry, [], shapes)[0]


def mix_second(kernel, pieces, order, carry, seen, field, direction, devices):
    rows, cols = seen.shape

    def finish(total, seen_ref, field_ref, direction_ref, image_ref, sums_ref):
        part = 128
        product = jnp.zeros((8, cols), F32)
        for m in range(0, rows, part):
            at = slice(m, m + part)
            image = seen_ref[at].astype(F32) * total[at] + field_ref[at]
            image_ref[at] = image
            terms = direction_ref[at] * image
            product += jnp.sum(terms.reshape(part // 8, 8, cols), axis=0)
        sums_ref[...] = jnp.broadcast_to(lanes([jnp.sum(product)])[None], sums_ref.shape)

    shapes = [
        jax.ShapeDtypeStruct((rows, cols), F32),
        jax.ShapeDtypeStruct((devices, 1, 128), F32),
    ]
    return mix(kernel, pieces, order, finish, carry, [seen, field, direction], shapes)


def fetch(order_ref, strip_refs, held, sems):
    copies = []
    for t in range(held.shape[0]):
        for side, strip_ref in enumerate(strip_refs):
            here = order_ref[0] if side == 0 else 1 - order_ref[0]
            target = held.at[t, here]
            copies.append(pltpu.make_async_copy(strip_ref.at[t], target, sems.at[t, side]))
    for copy in copies:
        copy.start()
    return copies


def multiply(left_ref, copies, held, total):
    total[...] = jnp.zeros_like(total)
    count = left_ref.shape[0]
    cols = held.shape[3] // STRIP
    for t in range(count):
        for side in range(2):
            copies[2 * t + side].wait()
        for r in range(STRIP):
            other = (t + r) % count
            at = slice(r * cols, (r + 1) * cols)
            block = jnp.concatenate([held[t, 0, :, at], held[t, 1, :, at]], axis=0)
            total[other] += jnp.dot(left_ref[t], block, preferred_element_type=F32)
            if 0 < r < STRIP - 1:
                total[t] += lax.dot_general(
                    left_ref[other], block, (((1,), (1,)), ((), ())), preferred_element_type=F32
                )


def cross_call(body, size, operands, strips, shapes, scratch):
    count, part, cols = size
    return pl.pallas_call(
        body,
        out_shape=shapes,
        in_specs=[SMEM if x.ndim == 1 else VMEM for x in operands] + [HBM] * len(strips),
        out_specs=[VMEM] * len(shapes),
        scratch_shapes=scratch
        + [
            pltpu.VMEM((count, part, cols), F32),
            pltpu.VMEM((count, 2) + strips[0].shape[1:], BF16),
            pltpu.SemaphoreType.DMA((count, 2)),
        ],
        compiler_params=pltpu.CompilerParams(vmem_limit_bytes=14 << 20),
        cost_estimate=pl.CostEstimate(
            flops=2 * part * (count * cols) ** 2,
            bytes_accessed=2 * (count * cols) ** 2,
            transcendentals=0,
        ),
    )(*operands, *in_hbm(strips))


def cross_first(order, mixed, slabs, strips, total_rows, devices):
    count, part, cols = mixed.shape

    def body(order_ref, mixed_ref, slab_ref, *refs):
        image_ref, sums_ref, total, held, sems = refs[2:]
        multiply(mixed_ref, fetch(order_ref, refs[:2], held, sems), held, total)
        sums = [jnp.zeros((part, cols), F32) for _ in range(3)]
        line = lax.broadcasted_iota(jnp.int32, (part, cols), 0)
        first = order_ref[1]
        for t in range(count):
            right = right_of(slab_ref, t, part)
            extra = slab_ref[t, 3 * part :].astype(F32)
            coef = extra[0:1] + extra[1:2] + extra[2:3]
            length = extra[3:4]
            above = jnp.where(line == 0, extra[4:5] + extra[5:6], pltpu.roll(right, 1, 0))
            below = jnp.where(
                line == part - 1, extra[6:7] + extra[7:8], pltpu.roll(right, part - 1, 0)
            )
            flux = linked(first + line, length, total_rows) * (below - right)
            flux -= linked(first + line - 1, length, total_rows) * (right - above)
            image = seen_of(slab_ref, t, part) * total[t] + (right - coef * flux)
            image_ref[t] = image
            terms = (right * right, right * image, image * image)
            sums = [a + b for a, b in zip(sums, terms)]
        row = lanes([jnp.sum(total) for total in sums])
        sums_ref[...] = jnp.broadcast_to(row[None], sums_ref.shape)

    shapes = [
        jax.ShapeDtypeStruct(mixed.shape, F32),
        jax.ShapeDtypeStruct((devices, 1, 128), F32),
    ]
    return cross_call(body, mixed.shape, [order, mixed, slabs], strips, shapes, [])


def cross_second(order, sums, slabs, image, strips):
    count, part, cols = image.shape

    def body(order_ref, sums_ref, slab_ref, image_ref, *refs):
        out_ref, factor_ref, left, total, held, sems = refs[2:]
        copies = fetch(order_ref, refs[:2], held, sems)
        sums = jnp.sum(sums_ref[...], axis=0)
        rr, ri, ii = sums[:, 0:1], sums[:, 1:2], sums[:, 2:3]
        alpha = rr / ri
        new = rr - 2.0 * alpha * ri + alpha * alpha * ii
        beta = new / rr
        factor_ref[...] = lanes([alpha, beta, new])
        for t in range(count):
            right = right_of(slab_ref, t, part)
            direction = right - alpha * image_ref[t] + beta * right
            left[t] = (seen_of(slab_ref, t, part) * direction).astype(BF16)
        multiply(left, copies, held, total)
        for t in range(count):
            out_ref[t] = total[t].astype(BF16)

    shapes = [
        jax.ShapeDtypeStruct(image.shape, BF16),
        jax.ShapeDtypeStruct((1, 128), F32),
    ]
    scratch = [pltpu.VMEM(image.shape, BF16)]
    return cross_call(body, image.shape, [order, sums, slabs, image], strips, shapes, scratch)


def conclude(sums, factors, right, direction, residual, image):
    rows, cols = right.shape

    def body(sums_ref, factor_ref, right_ref, direction_ref, residual_ref, image_ref, *outs):
        product = jnp.sum(sums_ref[...], axis=0)[:, 0:1]
        alpha, new = factor_ref[:, 0:1], factor_ref[:, 2:3]
        step = new / product
        part = 128
        for m in range(0, rows, part):
            at = slice(m, m + part)
            field = alpha * right_ref[at] + step * direction_ref[at]
            outs[0][at] = field[:, None, :]
            outs[1][at] = (residual_ref[at] - step * image_ref[at])[:, None, :]

    return pl.pallas_call(
        body,
        out_shape=[jax.ShapeDtypeStruct((rows, 1, cols), F32)] * 2,
        in_specs=[VMEM] * 6,
        out_specs=[VMEM] * 2,
        compiler_params=pltpu.CompilerParams(vmem_limit_bytes=10 << 20),
    )(sums, factors, right, direction, residual, image)


def linked(position, length, total_rows):
    later = (position + 1).astype(F32)
    whole_rows = jnp.floor((later + 0.5) / length) * length
    keep = (position >= 0) & (position + 1 < total_rows) & (later != whole_rows)
    return jnp.where(keep, 1.0, 0.0)


def field_of(cells, above, below, links, coef):
    padded = jnp.concatenate([above, cells, below], axis=-2)
    flux = links * (padded[..., 1:, :] - padded[..., :-1, :])
    return cells - coef * (flux[..., 1:, :] - flux[..., :-1, :])


def on_device(right_side, observed, row_length, field_coef, kernel_geno, kernel_trial):
    count = lax.axis_size("trial")
    rows, cols = observed.shape
    part = rows // count
    genos = lax.axis_size("geno")
    total_rows = rows * genos
    geno, trial = lax.axis_index("geno"), lax.axis_index("trial")
    right = right_side[:, 0, :]
    seen = observed.astype(F32)

    core = geno % CORES
    devices = count * genos
    following = [(i, i + 1) for i in range(genos - 1)]
    previous = [(i + 1, i) for i in range(genos - 1)]
    above = lax.ppermute(right[-1:], "geno", following)
    below = lax.ppermute(right[:1], "geno", previous)
    slabs = pack(count, right, observed, field_coef[None], row_length[None], above, below)
    strip = strip_of(core, trial, kernel_trial)
    strips = lax.all_gather(strip, "trial", axis=0)
    gathered, (slabs,) = gather_geno(
        (seen * right).astype(BF16), kernel_geno, slabs, spread=True
    )
    mixed, strips = together(mix_part(*gathered, BF16), strips)
    mixed_r = swap(mixed.reshape(count, part, cols))
    strips = [strips, hop(strips, core=1)]
    order = jnp.stack([core, geno * rows + trial * part]).astype(jnp.int32)

    image_r, sums = cross_first(order, mixed_r, slabs, strips, total_rows, devices)
    turned, factors = cross_second(order, exchange(sums), slabs, image_r, strips)
    turned, image_r = together(swap(turned), image_r)
    gathered, (image,) = gather_geno(turned.reshape(rows, cols), kernel_geno, swap(image_r))

    alpha, beta, new = factors[:, 0:1], factors[:, 1:2], factors[:, 2:3]
    image = image.reshape(rows, cols)
    residual = right - alpha * image
    direction = residual + beta * right
    above = lax.ppermute(direction[-1:], "geno", following)
    below = lax.ppermute(direction[:1], "geno", previous)
    position = (geno * rows - 1 + lax.iota(jnp.int32, rows + 1))[:, None]
    links = linked(position, row_length[None].astype(F32), total_rows)
    field = field_of(direction, above, below, links, field_coef[None])
    image, sums = mix_second(*gathered, seen.astype(BF16), field, direction, devices)
    return conclude(exchange(sums), factors, right, direction, residual, image)


def solution(mesh):
    return jax.shard_map(
        on_device,
        mesh=mesh,
        in_specs=(
            P("geno", None, "trial"),
            P("geno", "trial"),
            P("trial"),
            P("trial"),
            P("geno", None),
            P("trial", None),
        ),
        out_specs=(P("geno", None, "trial"), P("geno", None, "trial")),
        check_vma=False,
    )
```

```python
import jax
import jax.numpy as jnp
from jax import lax
from jax.experimental import pallas as pl
from jax.experimental.pallas import tpu as pltpu
from jax.sharding import PartitionSpec as P

BOTH = ("geno", "trial")
RING, PAIR, CORES = 4, 2, 2
F32, BF16 = jnp.float32, jnp.bfloat16
SMEM = pl.BlockSpec(memory_space=pltpu.SMEM)
VMEM = pl.BlockSpec(memory_space=pltpu.VMEM)
HBM = pl.BlockSpec(memory_space=pltpu.HBM)


def place(index):
    geno, trial = divmod(index, RING * PAIR)
    return (geno // 4, geno // 2 % 2, geno % 2, trial // 2, trial % 2)


def hop(cells, **by):
    step = [by.get(name, 0) for name in ("y", "z", "core", "x", "far")]
    pairs = []
    for index in range(RING * PAIR * CORES * RING * PAIR):
        y, z, core, x, far = (a + b for a, b in zip(place(index), step))
        geno = ((y % RING) * PAIR + z % PAIR) * CORES + core % CORES
        pairs.append((index, geno * RING * PAIR + (x % RING) * PAIR + far % PAIR))
    return lax.ppermute(cells, BOTH, pairs)


def together(*arrays):
    return lax.optimization_barrier(arrays)


STEPS = [(0, 0), (0, 1), (1, 0), (-1, 0), (2, 0), (1, 1), (-1, 1), (2, 1)]


def gather_geno(cells, kernel, *waiting, spread=False):
    geno = lax.axis_index("geno")
    y, z, core = geno // 4, geno // 2 % 2, geno % 2
    side, up = hop(cells, z=1), hop(cells, y=1)
    down, across = hop(cells, y=-1), hop(cells, y=2)
    side, up, down, across, kernel, *waiting = together(side, up, down, across, kernel, *waiting)
    if spread:
        waiting = [swap(cells) for cells in waiting]
        side_across = hop(side, y=2)
    else:
        side_across = hop(across, z=1)
    side_up, side_down = hop(side, y=1), hop(side, y=-1)
    others = [hop(piece, core=1) for piece in (cells, side, up, down, across)]
    order = []
    for a, b in STEPS:
        base = (((y - a) % RING) * PAIR + (z + b) % PAIR) * CORES
        order += [base + core, base + 1 - core]
    order = jnp.stack(order).astype(jnp.int32)
    pieces = [cells, others[0], side, others[1], up, others[2], down, others[3], across, others[4]]
    carry = mix_part(kernel, pieces, order[:10], None, F32)
    if not spread:
        image, edges = waiting[0], waiting[1:]
        carry, image = together(carry, image)
        following = [(i, i + 1) for i in range(RING * PAIR * CORES - 1)]
        previous = [(i + 1, i) for i in range(RING * PAIR * CORES - 1)]
        waiting = [
            lax.ppermute(edges[0], "geno", following),
            lax.ppermute(edges[1], "geno", previous),
        ]
    carry, side_up, side_down, side_across, *waiting = together(
        carry, side_up, side_down, side_across, *waiting
    )
    if not spread:
        waiting = [image, *waiting]
    pieces = []
    for piece in (side_up, side_down, side_across):
        pieces += [piece, hop(piece, core=1)]
    if spread:
        pieces[0], *waiting = together(pieces[0], *waiting)
    return (kernel, pieces, order[10:], carry), waiting


STRIP = 5


def split(values, count):
    terms = []
    for _ in range(count):
        terms.append(values.astype(BF16))
        values = values - terms[-1].astype(F32)
    return terms


def strip_of(core, trial, kernel):
    half, width = kernel.shape[0] // 2, STRIP * kernel.shape[0]
    rows = lax.dynamic_slice_in_dim(kernel, core * half, half, axis=0)
    rows = jnp.concatenate([rows, rows[:, : width - kernel.shape[0]]], axis=1)
    return lax.dynamic_slice_in_dim(rows, trial * kernel.shape[0], width, axis=1)


def pack(count, right, observed, coef, length, above, below):
    rows, cols = right.shape
    part = rows // count

    def body(right_ref, seen_ref, coef_ref, length_ref, above_ref, below_ref, out_ref):
        line = lax.broadcasted_iota(jnp.int32, (16, cols), 0)

        def put(extra, first, values, terms):
            for k in range(terms):
                term = values.astype(BF16).astype(F32)
                extra = jnp.where(line == first + k, term, extra)
                values = values - term
            return extra

        common = put(jnp.zeros((16, cols), F32), 0, coef_ref[...], 3)
        common = put(common, 3, length_ref[...].astype(F32), 1)
        for t in range(count):
            first, last = t * part, (t + 1) * part
            before = right_ref[first - 1 : first] if t else above_ref[...]
            behind = right_ref[last : last + 1] if last < rows else below_ref[...]
            extra = put(put(common, 4, before, 2), 6, behind, 2)
            high, low = split(right_ref[first:last], 2)
            seen = seen_ref[first:last].astype(F32).astype(BF16)
            for k, piece in enumerate((high, low, seen, extra.astype(BF16))):
                out_ref[t, k * part : k * part + piece.shape[0]] = piece

    return pl.pallas_call(
        body,
        out_shape=jax.ShapeDtypeStruct((count, 3 * part + 16, cols), BF16),
        in_specs=[VMEM] * 6,
        out_specs=VMEM,
        compiler_params=pltpu.CompilerParams(vmem_limit_bytes=10 << 20),
    )(right, observed, coef, length, above, below)


def right_of(slab_ref, t, part):
    return slab_ref[t, :part].astype(F32) + slab_ref[t, part : 2 * part].astype(F32)


def seen_of(slab_ref, t, part):
    return slab_ref[t, 2 * part : 3 * part].astype(F32)


def swap(slabs):
    return lax.all_to_all(slabs, "trial", split_axis=0, concat_axis=0, tiled=True)


def exchange(rows):
    return lax.all_to_all(rows, BOTH, 0, 0, tiled=True)


def lanes(values):
    lane = lax.broadcasted_iota(jnp.int32, (1, 128), 1)
    row = jnp.zeros((1, 128), F32)
    for k, value in enumerate(values):
        row = jnp.where(lane == k, value, row)
    return row


def in_hbm(arrays):
    return [pltpu.with_memory_space_constraint(cells, pltpu.HBM) for cells in arrays]


def mix(kernel, pieces, order, finish, carry, others, shapes):
    count = len(pieces)
    rows, cols = pieces[0].shape
    others = ([] if carry is None else [carry]) + others

    def body(order_ref, kernel_ref, *refs):
        piece_refs, rest = refs[:count], refs[count:-4]
        blocks, cells, total, sems = refs[-4:]
        copies = []
        for k in range(count):
            at = pl.ds(pl.multiple_of(order_ref[k] * rows, rows), rows)
            copies.append(
                (
                    pltpu.make_async_copy(kernel_ref.at[:, at], blocks.at[k], sems.at[k, 0]),
                    pltpu.make_async_copy(piece_refs[k], cells.at[k], sems.at[k, 1]),
                )
            )
        for pair in copies:
            for copy in pair:
                copy.start()
        if carry is not None:
            total[...] = rest[0][...]
            rest = rest[1:]
        for k in range(count):
            for copy in copies[k]:
                copy.wait()
            for m in range(0, rows, 256):
                term = jnp.dot(blocks[k, m : m + 256], cells[k], preferred_element_type=F32)
                if carry is None and k == 0:
                    total[m : m + 256] = term
                else:
                    total[m : m + 256] += term
        finish(total, *rest)

    return pl.pallas_call(
        body,
        out_shape=shapes,
        in_specs=[SMEM] + [HBM] * (1 + count) + [VMEM] * len(others),
        out_specs=[VMEM] * len(shapes),
        scratch_shapes=[
            pltpu.VMEM((count, rows, rows), BF16),
            pltpu.VMEM((count, rows, cols), BF16),
            pltpu.VMEM((rows, cols), F32),
            pltpu.SemaphoreType.DMA((count, 2)),
        ],
        compiler_params=pltpu.CompilerParams(vmem_limit_bytes=26 << 20),
    )(order, *in_hbm([kernel, *pieces]), *others)


def mix_part(kernel, pieces, order, carry, kind):
    def finish(total, out_ref):
        out_ref[...] = total[...].astype(kind)

    shapes = [jax.ShapeDtypeStruct(pieces[0].shape, kind)]
    return mix(kernel, pieces, order, finish, carry, [], shapes)[0]


def mix_second(kernel, pieces, order, carry, seen, field, direction, devices):
    rows, cols = seen.shape

    def finish(total, seen_ref, field_ref, direction_ref, image_ref, sums_ref):
        part = 128
        product = jnp.zeros((8, cols), F32)
        for m in range(0, rows, part):
            at = slice(m, m + part)
            image = seen_ref[at].astype(F32) * total[at] + field_ref[at]
            image_ref[at] = image
            terms = direction_ref[at] * image
            product += jnp.sum(terms.reshape(part // 8, 8, cols), axis=0)
        sums_ref[...] = jnp.broadcast_to(lanes([jnp.sum(product)])[None], sums_ref.shape)

    shapes = [
        jax.ShapeDtypeStruct((rows, cols), F32),
        jax.ShapeDtypeStruct((devices, 1, 128), F32),
    ]
    return mix(kernel, pieces, order, finish, carry, [seen, field, direction], shapes)


def fetch(order_ref, strip_refs, held, sems):
    copies = []
    for t in range(held.shape[0]):
        for side, strip_ref in enumerate(strip_refs):
            here = order_ref[0] if side == 0 else 1 - order_ref[0]
            target = held.at[t, here]
            copies.append(pltpu.make_async_copy(strip_ref.at[t], target, sems.at[t, side]))
    for copy in copies:
        copy.start()
    return copies


def multiply(left_ref, copies, held, total):
    total[...] = jnp.zeros_like(total)
    count = left_ref.shape[0]
    cols = held.shape[3] // STRIP
    for t in range(count):
        for side in range(2):
            copies[2 * t + side].wait()
        for r in range(STRIP):
            other = (t + r) % count
            at = slice(r * cols, (r + 1) * cols)
            block = jnp.concatenate([held[t, 0, :, at], held[t, 1, :, at]], axis=0)
            total[other] += jnp.dot(left_ref[t], block, preferred_element_type=F32)
            if 0 < r < STRIP - 1:
                total[t] += lax.dot_general(
                    left_ref[other], block, (((1,), (1,)), ((), ())), preferred_element_type=F32
                )


def cross_call(body, size, operands, strips, shapes, scratch):
    count, part, cols = size
    return pl.pallas_call(
        body,
        out_shape=shapes,
        in_specs=[SMEM if x.ndim == 1 else VMEM for x in operands] + [HBM] * len(strips),
        out_specs=[VMEM] * len(shapes),
        scratch_shapes=scratch
        + [
            pltpu.VMEM((count, part, cols), F32),
            pltpu.VMEM((count, 2) + strips[0].shape[1:], BF16),
            pltpu.SemaphoreType.DMA((count, 2)),
        ],
        compiler_params=pltpu.CompilerParams(vmem_limit_bytes=14 << 20),
        cost_estimate=pl.CostEstimate(
            flops=2 * part * (count * cols) ** 2,
            bytes_accessed=2 * (count * cols) ** 2,
            transcendentals=0,
        ),
    )(*operands, *in_hbm(strips))


def cross_first(order, mixed, slabs, strips, total_rows, devices):
    count, part, cols = mixed.shape

    def body(order_ref, mixed_ref, slab_ref, *refs):
        image_ref, sums_ref, total, held, sems = refs[2:]
        multiply(mixed_ref, fetch(order_ref, refs[:2], held, sems), held, total)
        sums = [jnp.zeros((part, cols), F32) for _ in range(3)]
        line = lax.broadcasted_iota(jnp.int32, (part, cols), 0)
        first = order_ref[1]
        for t in range(count):
            right = right_of(slab_ref, t, part)
            extra = slab_ref[t, 3 * part :].astype(F32)
            coef = extra[0:1] + extra[1:2] + extra[2:3]
            length = extra[3:4]
            above = jnp.where(line == 0, extra[4:5] + extra[5:6], pltpu.roll(right, 1, 0))
            below = jnp.where(
                line == part - 1, extra[6:7] + extra[7:8], pltpu.roll(right, part - 1, 0)
            )
            flux = linked(first + line, length, total_rows) * (below - right)
            flux -= linked(first + line - 1, length, total_rows) * (right - above)
            image = seen_of(slab_ref, t, part) * total[t] + (right - coef * flux)
            image_ref[t] = image
            terms = (right * right, right * image, image * image)
            sums = [a + b for a, b in zip(sums, terms)]
        row = lanes([jnp.sum(total) for total in sums])
        sums_ref[...] = jnp.broadcast_to(row[None], sums_ref.shape)

    shapes = [
        jax.ShapeDtypeStruct(mixed.shape, F32),
        jax.ShapeDtypeStruct((devices, 1, 128), F32),
    ]
    return cross_call(body, mixed.shape, [order, mixed, slabs], strips, shapes, [])


def cross_second(order, sums, slabs, image, strips):
    count, part, cols = image.shape

    def body(order_ref, sums_ref, slab_ref, image_ref, *refs):
        out_ref, factor_ref, left, total, held, sems = refs[2:]
        copies = fetch(order_ref, refs[:2], held, sems)
        sums = jnp.sum(sums_ref[...], axis=0)
        rr, ri, ii = sums[:, 0:1], sums[:, 1:2], sums[:, 2:3]
        alpha = rr / ri
        new = rr - 2.0 * alpha * ri + alpha * alpha * ii
        beta = new / rr
        factor_ref[...] = lanes([alpha, beta, new])
        for t in range(count):
            right = right_of(slab_ref, t, part)
            direction = right - alpha * image_ref[t] + beta * right
            left[t] = (seen_of(slab_ref, t, part) * direction).astype(BF16)
        multiply(left, copies, held, total)
        for t in range(count):
            out_ref[t] = total[t].astype(BF16)

    shapes = [
        jax.ShapeDtypeStruct(image.shape, BF16),
        jax.ShapeDtypeStruct((1, 128), F32),
    ]
    scratch = [pltpu.VMEM(image.shape, BF16)]
    return cross_call(body, image.shape, [order, sums, slabs, image], strips, shapes, scratch)


def conclude(sums, factors, right, direction, residual, image):
    rows, cols = right.shape

    def body(sums_ref, factor_ref, right_ref, direction_ref, residual_ref, image_ref, *outs):
        product = jnp.sum(sums_ref[...], axis=0)[:, 0:1]
        alpha, new = factor_ref[:, 0:1], factor_ref[:, 2:3]
        step = new / product
        part = 128
        for m in range(0, rows, part):
            at = slice(m, m + part)
            field = alpha * right_ref[at] + step * direction_ref[at]
            outs[0][at] = field[:, None, :]
            outs[1][at] = (residual_ref[at] - step * image_ref[at])[:, None, :]

    return pl.pallas_call(
        body,
        out_shape=[jax.ShapeDtypeStruct((rows, 1, cols), F32)] * 2,
        in_specs=[VMEM] * 6,
        out_specs=[VMEM] * 2,
        compiler_params=pltpu.CompilerParams(vmem_limit_bytes=10 << 20),
    )(sums, factors, right, direction, residual, image)


def linked(position, length, total_rows):
    later = (position + 1).astype(F32)
    whole_rows = jnp.floor((later + 0.5) / length) * length
    keep = (position >= 0) & (position + 1 < total_rows) & (later != whole_rows)
    return jnp.where(keep, 1.0, 0.0)


def field_of(cells, above, below, links, coef):
    padded = jnp.concatenate([above, cells, below], axis=-2)
    flux = links * (padded[..., 1:, :] - padded[..., :-1, :])
    return cells - coef * (flux[..., 1:, :] - flux[..., :-1, :])


def on_device(right_side, observed, row_length, field_coef, kernel_geno, kernel_trial):
    count = lax.axis_size("trial")
    rows, cols = observed.shape
    part = rows // count
    genos = lax.axis_size("geno")
    total_rows = rows * genos
    geno, trial = lax.axis_index("geno"), lax.axis_index("trial")
    right = right_side[:, 0, :]
    seen = observed.astype(F32)

    core = geno % CORES
    devices = count * genos
    following = [(i, i + 1) for i in range(genos - 1)]
    previous = [(i + 1, i) for i in range(genos - 1)]
    above = lax.ppermute(right[-1:], "geno", following)
    below = lax.ppermute(right[:1], "geno", previous)
    slabs = pack(count, right, observed, field_coef[None], row_length[None], above, below)
    strip = strip_of(core, trial, kernel_trial)
    strips = lax.all_gather(strip, "trial", axis=0)
    gathered, (slabs,) = gather_geno(
        (seen * right).astype(BF16), kernel_geno, slabs, spread=True
    )
    mixed, strips = together(mix_part(*gathered, BF16), strips)
    mixed_r = swap(mixed.reshape(count, part, cols))
    strips = [strips, hop(strips, core=1)]
    order = jnp.stack([core, geno * rows + trial * part]).astype(jnp.int32)

    image_r, sums = cross_first(order, mixed_r, slabs, strips, total_rows, devices)
    turned, factors = cross_second(order, exchange(sums), slabs, image_r, strips)
    turned, image_r = together(swap(turned), image_r)
    alpha, beta, new = factors[:, 0:1], factors[:, 1:2], factors[:, 2:3]
    image = swap(image_r)
    last, first = image[-1, -1:], image[0, :1]
    last = right[-1:] - alpha * last + beta * right[-1:]
    first = right[:1] - alpha * first + beta * right[:1]
    gathered, (image, above, below) = gather_geno(
        turned.reshape(rows, cols), kernel_geno, image, last, first
    )

    image = image.reshape(rows, cols)
    residual = right - alpha * image
    direction = residual + beta * right
    position = (geno * rows - 1 + lax.iota(jnp.int32, rows + 1))[:, None]
    links = linked(position, row_length[None].astype(F32), total_rows)
    field = field_of(direction, above, below, links, field_coef[None])
    image, sums = mix_second(*gathered, seen.astype(BF16), field, direction, devices)
    return conclude(exchange(sums), factors, right, direction, residual, image)


def solution(mesh):
    return jax.shard_map(
        on_device,
        mesh=mesh,
        in_specs=(
            P("geno", None, "trial"),
            P("geno", "trial"),
            P("trial"),
            P("trial"),
            P("geno", None),
            P("trial", None),
        ),
        out_specs=(P("geno", None, "trial"), P("geno", None, "trial")),
        check_vma=False,
    )
```

```python
import jax
import jax.numpy as jnp
from jax import lax
from jax.experimental import pallas as pl
from jax.experimental.pallas import tpu as pltpu
from jax.sharding import PartitionSpec as P

BOTH = ("geno", "trial")
RING, PAIR, CORES = 4, 2, 2
F32, BF16 = jnp.float32, jnp.bfloat16
SMEM = pl.BlockSpec(memory_space=pltpu.SMEM)
VMEM = pl.BlockSpec(memory_space=pltpu.VMEM)
HBM = pl.BlockSpec(memory_space=pltpu.HBM)


def place(index):
    geno, trial = divmod(index, RING * PAIR)
    return (geno // 4, geno // 2 % 2, geno % 2, trial // 2, trial % 2)


def hop(cells, **by):
    step = [by.get(name, 0) for name in ("y", "z", "core", "x", "far")]
    pairs = []
    for index in range(RING * PAIR * CORES * RING * PAIR):
        y, z, core, x, far = (a + b for a, b in zip(place(index), step))
        geno = ((y % RING) * PAIR + z % PAIR) * CORES + core % CORES
        pairs.append((index, geno * RING * PAIR + (x % RING) * PAIR + far % PAIR))
    return lax.ppermute(cells, BOTH, pairs)


def together(*arrays):
    return lax.optimization_barrier(arrays)


STEPS = [(0, 0), (0, 1), (1, 0), (-1, 0), (2, 0), (1, 1), (-1, 1), (2, 1)]


def gather_geno(cells, kernel, *waiting, spread=False):
    geno = lax.axis_index("geno")
    y, z, core = geno // 4, geno // 2 % 2, geno % 2
    side, up = hop(cells, z=1), hop(cells, y=1)
    down, across = hop(cells, y=-1), hop(cells, y=2)
    side, up, down, across, kernel, *waiting = together(side, up, down, across, kernel, *waiting)
    if spread:
        waiting = [swap(cells) for cells in waiting]
        side_across = hop(side, y=2)
    else:
        side_across = hop(across, z=1)
    side_up, side_down = hop(side, y=1), hop(side, y=-1)
    others = [hop(piece, core=1) for piece in (cells, side, up, down, across)]
    order = []
    for a, b in STEPS:
        base = (((y - a) % RING) * PAIR + (z + b) % PAIR) * CORES
        order += [base + core, base + 1 - core]
    order = jnp.stack(order).astype(jnp.int32)
    pieces = [cells, others[0], side, others[1], up, others[2], down, others[3], across, others[4]]
    carry = mix_part(kernel, pieces, order[:10], None, F32)
    if not spread:
        image, edges = waiting[0], waiting[1:]
        carry, image = together(carry, image)
        following = [(i, i + 1) for i in range(RING * PAIR * CORES - 1)]
        previous = [(i + 1, i) for i in range(RING * PAIR * CORES - 1)]
        waiting = [
            lax.ppermute(edges[0], "geno", following),
            lax.ppermute(edges[1], "geno", previous),
        ]
    carry, side_up, side_down, side_across, *waiting = together(
        carry, side_up, side_down, side_across, *waiting
    )
    if not spread:
        waiting = [image, *waiting]
    pieces = []
    for piece in (side_up, side_down, side_across):
        pieces += [piece, hop(piece, core=1)]
    if spread:
        pieces[0], *waiting = together(pieces[0], *waiting)
    return (kernel, pieces, order[10:], carry), waiting


STRIP = 5


def split(values, count):
    terms = []
    for _ in range(count):
        terms.append(values.astype(BF16))
        values = values - terms[-1].astype(F32)
    return terms


def strip_of(core, trial, kernel):
    half, width = kernel.shape[0] // 2, STRIP * kernel.shape[0]
    rows = lax.dynamic_slice_in_dim(kernel, core * half, half, axis=0)
    rows = jnp.concatenate([rows, rows[:, : width - kernel.shape[0]]], axis=1)
    return lax.dynamic_slice_in_dim(rows, trial * kernel.shape[0], width, axis=1)


def pack(count, right, observed, coef, length, above, below):
    rows, cols = right.shape
    part = rows // count

    def body(right_ref, seen_ref, coef_ref, length_ref, above_ref, below_ref, out_ref):
        line = lax.broadcasted_iota(jnp.int32, (16, cols), 0)

        def put(extra, first, values, terms):
            for k in range(terms):
                term = values.astype(BF16).astype(F32)
                extra = jnp.where(line == first + k, term, extra)
                values = values - term
            return extra

        common = put(jnp.zeros((16, cols), F32), 0, coef_ref[...], 3)
        common = put(common, 3, length_ref[...].astype(F32), 1)
        for t in range(count):
            first, last = t * part, (t + 1) * part
            before = right_ref[first - 1 : first] if t else above_ref[...]
            behind = right_ref[last : last + 1] if last < rows else below_ref[...]
            extra = put(put(common, 4, before, 2), 6, behind, 2)
            high, low = split(right_ref[first:last], 2)
            seen = seen_ref[first:last].astype(F32).astype(BF16)
            for k, piece in enumerate((high, low, seen, extra.astype(BF16))):
                out_ref[t, k * part : k * part + piece.shape[0]] = piece

    return pl.pallas_call(
        body,
        out_shape=jax.ShapeDtypeStruct((count, 3 * part + 16, cols), BF16),
        in_specs=[VMEM] * 6,
        out_specs=VMEM,
        compiler_params=pltpu.CompilerParams(vmem_limit_bytes=10 << 20),
    )(right, observed, coef, length, above, below)


def right_of(slab_ref, t, part):
    return slab_ref[t, :part].astype(F32) + slab_ref[t, part : 2 * part].astype(F32)


def seen_of(slab_ref, t, part):
    return slab_ref[t, 2 * part : 3 * part].astype(F32)


def swap(slabs):
    return lax.all_to_all(slabs, "trial", split_axis=0, concat_axis=0, tiled=True)


def exchange(rows):
    return lax.all_to_all(rows, BOTH, 0, 0, tiled=True)


def lanes(values):
    lane = lax.broadcasted_iota(jnp.int32, (1, 128), 1)
    row = jnp.zeros((1, 128), F32)
    for k, value in enumerate(values):
        row = jnp.where(lane == k, value, row)
    return row


def in_hbm(arrays):
    return [pltpu.with_memory_space_constraint(cells, pltpu.HBM) for cells in arrays]


def mix(kernel, pieces, order, finish, carry, others, shapes):
    count = len(pieces)
    rows, cols = pieces[0].shape
    others = ([] if carry is None else [carry]) + others

    def body(order_ref, kernel_ref, *refs):
        piece_refs, rest = refs[:count], refs[count:-4]
        blocks, cells, total, sems = refs[-4:]
        copies = []
        for k in range(count):
            at = pl.ds(pl.multiple_of(order_ref[k] * rows, rows), rows)
            here = slice(k * rows, (k + 1) * rows)
            copies.append(
                (
                    pltpu.make_async_copy(kernel_ref.at[:, at], blocks.at[:, here], sems.at[k, 0]),
                    pltpu.make_async_copy(piece_refs[k], cells.at[here], sems.at[k, 1]),
                )
            )
        for pair in copies:
            for copy in pair:
                copy.start()
        if carry is not None:
            total[...] = rest[0][...]
            rest = rest[1:]
        for k in range(0, count, 2):
            for copy in copies[k] + copies[k + 1]:
                copy.wait()
            two = slice(k * rows, (k + 2) * rows)
            for m in range(0, rows, 256):
                term = jnp.dot(blocks[m : m + 256, two], cells[two], preferred_element_type=F32)
                if carry is None and k == 0:
                    total[m : m + 256] = term
                else:
                    total[m : m + 256] += term
        finish(total, *rest)

    return pl.pallas_call(
        body,
        out_shape=shapes,
        in_specs=[SMEM] + [HBM] * (1 + count) + [VMEM] * len(others),
        out_specs=[VMEM] * len(shapes),
        scratch_shapes=[
            pltpu.VMEM((rows, count * rows), BF16),
            pltpu.VMEM((count * rows, cols), BF16),
            pltpu.VMEM((rows, cols), F32),
            pltpu.SemaphoreType.DMA((count, 2)),
        ],
        compiler_params=pltpu.CompilerParams(vmem_limit_bytes=26 << 20),
    )(order, *in_hbm([kernel, *pieces]), *others)


def mix_part(kernel, pieces, order, carry, kind):
    def finish(total, out_ref):
        out_ref[...] = total[...].astype(kind)

    shapes = [jax.ShapeDtypeStruct(pieces[0].shape, kind)]
    return mix(kernel, pieces, order, finish, carry, [], shapes)[0]


def mix_second(kernel, pieces, order, carry, seen, field, direction, devices):
    rows, cols = seen.shape

    def finish(total, seen_ref, field_ref, direction_ref, image_ref, sums_ref):
        part = 128
        product = jnp.zeros((8, cols), F32)
        for m in range(0, rows, part):
            at = slice(m, m + part)
            image = seen_ref[at].astype(F32) * total[at] + field_ref[at]
            image_ref[at] = image
            terms = direction_ref[at] * image
            product += jnp.sum(terms.reshape(part // 8, 8, cols), axis=0)
        sums_ref[...] = jnp.broadcast_to(lanes([jnp.sum(product)])[None], sums_ref.shape)

    shapes = [
        jax.ShapeDtypeStruct((rows, cols), F32),
        jax.ShapeDtypeStruct((devices, 1, 128), F32),
    ]
    return mix(kernel, pieces, order, finish, carry, [seen, field, direction], shapes)


def fetch(order_ref, strip_refs, held, sems):
    copies = []
    for t in range(held.shape[0]):
        for side, strip_ref in enumerate(strip_refs):
            here = order_ref[0] if side == 0 else 1 - order_ref[0]
            target = held.at[t, here]
            copies.append(pltpu.make_async_copy(strip_ref.at[t], target, sems.at[t, side]))
    for copy in copies:
        copy.start()
    return copies


def multiply(left_ref, copies, held, total):
    total[...] = jnp.zeros_like(total)
    count = left_ref.shape[0]
    cols = held.shape[3] // STRIP
    for t in range(count):
        for side in range(2):
            copies[2 * t + side].wait()
        for r in range(STRIP):
            other = (t + r) % count
            at = slice(r * cols, (r + 1) * cols)
            block = jnp.concatenate([held[t, 0, :, at], held[t, 1, :, at]], axis=0)
            total[other] += jnp.dot(left_ref[t], block, preferred_element_type=F32)
            if 0 < r < STRIP - 1:
                total[t] += lax.dot_general(
                    left_ref[other], block, (((1,), (1,)), ((), ())), preferred_element_type=F32
                )


def cross_call(body, size, operands, strips, shapes, scratch):
    count, part, cols = size
    return pl.pallas_call(
        body,
        out_shape=shapes,
        in_specs=[SMEM if x.ndim == 1 else VMEM for x in operands] + [HBM] * len(strips),
        out_specs=[VMEM] * len(shapes),
        scratch_shapes=scratch
        + [
            pltpu.VMEM((count, part, cols), F32),
            pltpu.VMEM((count, 2) + strips[0].shape[1:], BF16),
            pltpu.SemaphoreType.DMA((count, 2)),
        ],
        compiler_params=pltpu.CompilerParams(vmem_limit_bytes=14 << 20),
        cost_estimate=pl.CostEstimate(
            flops=2 * part * (count * cols) ** 2,
            bytes_accessed=2 * (count * cols) ** 2,
            transcendentals=0,
        ),
    )(*operands, *in_hbm(strips))


def cross_first(order, mixed, slabs, strips, total_rows, devices):
    count, part, cols = mixed.shape

    def body(order_ref, mixed_ref, slab_ref, *refs):
        image_ref, sums_ref, total, held, sems = refs[2:]
        multiply(mixed_ref, fetch(order_ref, refs[:2], held, sems), held, total)
        sums = [jnp.zeros((part, cols), F32) for _ in range(3)]
        line = lax.broadcasted_iota(jnp.int32, (part, cols), 0)
        first = order_ref[1]
        for t in range(count):
            right = right_of(slab_ref, t, part)
            extra = slab_ref[t, 3 * part :].astype(F32)
            coef = extra[0:1] + extra[1:2] + extra[2:3]
            length = extra[3:4]
            above = jnp.where(line == 0, extra[4:5] + extra[5:6], pltpu.roll(right, 1, 0))
            below = jnp.where(
                line == part - 1, extra[6:7] + extra[7:8], pltpu.roll(right, part - 1, 0)
            )
            flux = linked(first + line, length, total_rows) * (below - right)
            flux -= linked(first + line - 1, length, total_rows) * (right - above)
            image = seen_of(slab_ref, t, part) * total[t] + (right - coef * flux)
            image_ref[t] = image
            terms = (right * right, right * image, image * image)
            sums = [a + b for a, b in zip(sums, terms)]
        row = lanes([jnp.sum(total) for total in sums])
        sums_ref[...] = jnp.broadcast_to(row[None], sums_ref.shape)

    shapes = [
        jax.ShapeDtypeStruct(mixed.shape, F32),
        jax.ShapeDtypeStruct((devices, 1, 128), F32),
    ]
    return cross_call(body, mixed.shape, [order, mixed, slabs], strips, shapes, [])


def cross_second(order, sums, slabs, image, strips):
    count, part, cols = image.shape

    def body(order_ref, sums_ref, slab_ref, image_ref, *refs):
        out_ref, factor_ref, left, total, held, sems = refs[2:]
        copies = fetch(order_ref, refs[:2], held, sems)
        sums = jnp.sum(sums_ref[...], axis=0)
        rr, ri, ii = sums[:, 0:1], sums[:, 1:2], sums[:, 2:3]
        alpha = rr / ri
        new = rr - 2.0 * alpha * ri + alpha * alpha * ii
        beta = new / rr
        factor_ref[...] = lanes([alpha, beta, new])
        for t in range(count):
            right = right_of(slab_ref, t, part)
            direction = right - alpha * image_ref[t] + beta * right
            left[t] = (seen_of(slab_ref, t, part) * direction).astype(BF16)
        multiply(left, copies, held, total)
        for t in range(count):
            out_ref[t] = total[t].astype(BF16)

    shapes = [
        jax.ShapeDtypeStruct(image.shape, BF16),
        jax.ShapeDtypeStruct((1, 128), F32),
    ]
    scratch = [pltpu.VMEM(image.shape, BF16)]
    return cross_call(body, image.shape, [order, sums, slabs, image], strips, shapes, scratch)


def conclude(sums, factors, right, direction, residual, image):
    rows, cols = right.shape

    def body(sums_ref, factor_ref, right_ref, direction_ref, residual_ref, image_ref, *outs):
        product = jnp.sum(sums_ref[...], axis=0)[:, 0:1]
        alpha, new = factor_ref[:, 0:1], factor_ref[:, 2:3]
        step = new / product
        part = 128
        for m in range(0, rows, part):
            at = slice(m, m + part)
            field = alpha * right_ref[at] + step * direction_ref[at]
            outs[0][at] = field[:, None, :]
            outs[1][at] = (residual_ref[at] - step * image_ref[at])[:, None, :]

    return pl.pallas_call(
        body,
        out_shape=[jax.ShapeDtypeStruct((rows, 1, cols), F32)] * 2,
        in_specs=[VMEM] * 6,
        out_specs=[VMEM] * 2,
        compiler_params=pltpu.CompilerParams(vmem_limit_bytes=10 << 20),
    )(sums, factors, right, direction, residual, image)


def linked(position, length, total_rows):
    later = (position + 1).astype(F32)
    whole_rows = jnp.floor((later + 0.5) / length) * length
    keep = (position >= 0) & (position + 1 < total_rows) & (later != whole_rows)
    return jnp.where(keep, 1.0, 0.0)


def field_of(cells, above, below, links, coef):
    padded = jnp.concatenate([above, cells, below], axis=-2)
    flux = links * (padded[..., 1:, :] - padded[..., :-1, :])
    return cells - coef * (flux[..., 1:, :] - flux[..., :-1, :])


def on_device(right_side, observed, row_length, field_coef, kernel_geno, kernel_trial):
    count = lax.axis_size("trial")
    rows, cols = observed.shape
    part = rows // count
    genos = lax.axis_size("geno")
    total_rows = rows * genos
    geno, trial = lax.axis_index("geno"), lax.axis_index("trial")
    right = right_side[:, 0, :]
    seen = observed.astype(F32)

    core = geno % CORES
    devices = count * genos
    following = [(i, i + 1) for i in range(genos - 1)]
    previous = [(i + 1, i) for i in range(genos - 1)]
    above = lax.ppermute(right[-1:], "geno", following)
    below = lax.ppermute(right[:1], "geno", previous)
    slabs = pack(count, right, observed, field_coef[None], row_length[None], above, below)
    strip = strip_of(core, trial, kernel_trial)
    strips = lax.all_gather(strip, "trial", axis=0)
    gathered, (slabs,) = gather_geno(
        (seen * right).astype(BF16), kernel_geno, slabs, spread=True
    )
    mixed, strips = together(mix_part(*gathered, BF16), strips)
    mixed_r = swap(mixed.reshape(count, part, cols))
    strips = [strips, hop(strips, core=1)]
    order = jnp.stack([core, geno * rows + trial * part]).astype(jnp.int32)

    image_r, sums = cross_first(order, mixed_r, slabs, strips, total_rows, devices)
    turned, factors = cross_second(order, exchange(sums), slabs, image_r, strips)
    turned, image_r = together(swap(turned), image_r)
    alpha, beta, new = factors[:, 0:1], factors[:, 1:2], factors[:, 2:3]
    image = swap(image_r)
    last, first = image[-1, -1:], image[0, :1]
    last = right[-1:] - alpha * last + beta * right[-1:]
    first = right[:1] - alpha * first + beta * right[:1]
    gathered, (image, above, below) = gather_geno(
        turned.reshape(rows, cols), kernel_geno, image, last, first
    )

    image = image.reshape(rows, cols)
    residual = right - alpha * image
    direction = residual + beta * right
    position = (geno * rows - 1 + lax.iota(jnp.int32, rows + 1))[:, None]
    links = linked(position, row_length[None].astype(F32), total_rows)
    field = field_of(direction, above, below, links, field_coef[None])
    image, sums = mix_second(*gathered, seen.astype(BF16), field, direction, devices)
    return conclude(exchange(sums), factors, right, direction, residual, image)


def solution(mesh):
    return jax.shard_map(
        on_device,
        mesh=mesh,
        in_specs=(
            P("geno", None, "trial"),
            P("geno", "trial"),
            P("trial"),
            P("trial"),
            P("geno", None),
            P("trial", None),
        ),
        out_specs=(P("geno", None, "trial"), P("geno", None, "trial")),
        check_vma=False,
    )
```
